32 devices in a mesh: rows: 16 (over z, y, x), feat: 2 (over core).
Axes of the slice: x: 2, y: 2, z: 4, core: 2. Of those that a mesh axis runs over, the one named last changes fastest.
Arguments:
- descriptors: bfloat16 [4096, 128], P('rows'), may hold values from -6 to 6
- freqs: bfloat16 [128, 32768], P(None, 'feat'), may hold values from -0.5 to 0.5
- phases: float32 [32768], P('feat'), may hold values from -3.140625 to 3.140625
- row_weight: float32 [4096], P('rows'), may hold values from 0.3 to 15, as said below
- resid: float32 [4096, 128], P('rows'), may hold values from -6 to 6
- coef: float32 [32768, 128], P(('feat', 'rows')), may hold values from -4 to 4
- direction: float32 [32768, 128], P(('feat', 'rows')), may hold values from -6 to 6
- ridge: float32 [128], replicated, may hold values from 1 to 10
- gamma: float32 [128], replicated, may hold values from 300000 to 3000000
Outputs:
- coef_new: float32 [32768, 128], P(('feat', 'rows'))
- resid_new: float32 [4096, 128], P('rows')
- direction_new: float32 [32768, 128], P(('feat', 'rows'))
- gamma_new: float32 [128], replicated
The draws below stay inside these ranges and needn't reach their ends.
Inputs may be any that keep to these rules, and one draw needn't show every extreme that they name: `row_weight`: positive weights of the profile rows.
All inputs are finite; a program needn't handle non-finite values.
Results may differ from the reference program's by a relative error of at most 0.0006.
The reference program's roundings to bfloat16 on the way count: a program that leaves them out, or rounds other values in their place, can miss the bound.
Values may be sent and summed in bfloat16 or wider, within the bound.
A program may use at most 64 MiB of HBM per device.

```python
import math
import jax
import jax.numpy as jnp
from jax import lax

DESC = 128
TARGETS = 128
FEAT = 32768
ROWS = 4096


def draw_row_weight(key, part):
    ramp = 1.0 + 2.0 * jnp.arange(ROWS, dtype=jnp.float32) / max(ROWS - 1, 1)
    spread = jnp.exp(jax.random.uniform(key, (ROWS,), jnp.float32, 0.0, math.log(10.0)))
    return 0.3 * ramp * spread


def steps_of(own_key, dims, cuts, low, high):
    factor_of = 1.0
    for dim, shards_of in cuts:
        steps = jax.random.uniform(jax.random.fold_in(jax.random.fold_in(own_key, 6), dim), (shards_of,), jnp.float32, low / len(cuts), high / len(cuts))
        factor_of = factor_of * jnp.repeat(jnp.exp(steps), dims[dim] // shards_of).reshape((-1,) + (1,) * (len(dims) - 1 - dim))
    return factor_of


def centred(own_key, dims, scale, limit, split=(), kind=jnp.bfloat16):
    entries = scale * jax.random.normal(own_key, dims, jnp.float32)
    if split:
        entries = entries * steps_of(own_key, dims, split, -0.22, 0.18)
    return jnp.clip(entries, -limit, limit).astype(kind)


def setup_inputs(seed: int = 0) -> dict:
    arg_keys = jax.random.split(jax.random.key(seed), 10)
    return {
        "descriptors": centred(arg_keys[0], (ROWS, DESC), 1.0, 6.0, ((0, 16),)),
        "freqs": centred(arg_keys[1], (DESC, FEAT), DESC ** -0.5, 0.5, ((1, 2),)),
        "phases": jnp.clip(jax.random.uniform(arg_keys[2], (FEAT,), jnp.float32, -3.140625, 3.140625), -3.140625, 3.140625),
        "row_weight": draw_row_weight(jax.random.fold_in(arg_keys[9], 71), 0),
        "resid": centred(arg_keys[4], (ROWS, TARGETS), 1.0, 6.0, ((0, 16),), jnp.float32),
        "coef": centred(arg_keys[5], (FEAT, TARGETS), 0.3, 4.0, ((0, 32),), jnp.float32),
        "direction": centred(arg_keys[6], (FEAT, TARGETS), 1.0, 6.0, ((0, 32),), jnp.float32),
        "ridge": jnp.clip(jnp.exp(jax.random.uniform(arg_keys[7], (TARGETS,), jnp.float32, math.log(1.0), math.log(10.0))), 1.0, 10.0),
        "gamma": jnp.clip(jnp.exp(jax.random.uniform(arg_keys[8], (TARGETS,), jnp.float32, math.log(300000.0), math.log(3000000))), 300000.0, 3000000),
    }


def make_features(block_x, freqs, phases):
    scale = math.sqrt(2.0 / FEAT)
    angle = jnp.dot(block_x, freqs, preferred_element_type=jnp.float32) + phases[None, :]
    return (scale * jnp.cos(angle)).astype(jnp.bfloat16)

def reference(descriptors, freqs, phases, row_weight, resid, coef, direction, ridge, gamma):
    block = min(512, ROWS)
    count = ROWS // block
    stacked = descriptors.reshape(count, block, DESC)
    direction_b = direction.astype(jnp.bfloat16)

    def image_block(block_x):
        return jnp.dot(make_features(block_x, freqs, phases), direction_b, preferred_element_type=jnp.float32)
    summed = lax.map(image_block, stacked).reshape(ROWS, TARGETS)
    image = row_weight[:, None] * summed
    curvature = lax.optimization_barrier(jnp.sum(image * image, axis=0)) + ridge * lax.optimization_barrier(jnp.sum(direction * direction, axis=0))
    alpha = gamma / curvature
    coef_new = coef + alpha[None, :] * direction
    resid_new = resid - alpha[None, :] * image
    weighted_b = (row_weight[:, None] * resid_new).astype(jnp.bfloat16).reshape(count, block, TARGETS)

    def grad_step(total, pair):
        block_x, block_w = pair
        feats = make_features(block_x, freqs, phases)
        term = lax.dot_general(feats, block_w, (((0,), (0,)), ((), ())), preferred_element_type=jnp.float32)
        return (total + term, None)
    start = jnp.zeros((FEAT, TARGETS), jnp.float32)
    summed_grad, unused = lax.scan(grad_step, start, (stacked, weighted_b))
    gradient = summed_grad - ridge[None, :] * coef_new
    gamma_new = lax.optimization_barrier(jnp.sum(gradient * gradient, axis=0))
    direction_new = gradient + (gamma_new / gamma)[None, :] * direction
    return (coef_new, resid_new, direction_new, gamma_new)
```

```python
import math

import jax
import jax.numpy as jnp
from jax import lax
from jax.sharding import PartitionSpec as P

FEAT = 32768


def make_features(block_x, freq_cols, phase_cols):
    scale = math.sqrt(2.0 / FEAT)
    angle = jnp.dot(block_x, freq_cols, preferred_element_type=jnp.float32) + phase_cols[None, :]
    return (scale * jnp.cos(angle)).astype(jnp.bfloat16)


def body(descriptors, freqs, phases, row_weight, resid, coef, direction, ridge, gamma):
    own = coef.shape[0]
    groups = lax.axis_size("feat")
    start = lax.axis_index("rows") * own
    freq_cols = lax.dynamic_slice_in_dim(freqs, start, own, 1)
    phase_cols = lax.dynamic_slice_in_dim(phases, start, own, 0)
    every = lax.all_gather(descriptors, "rows", axis=0, tiled=True)
    feats = make_features(every, freq_cols, phase_cols)
    part = jnp.dot(feats, direction.astype(jnp.bfloat16), preferred_element_type=jnp.float32)
    part = lax.psum_scatter(part, "rows", scatter_dimension=0, tiled=True)
    image = row_weight[:, None] * lax.psum(part, "feat")
    sums = jnp.stack([jnp.sum(image * image, axis=0) / groups, jnp.sum(direction * direction, axis=0)])
    sums = lax.psum(sums, ("rows", "feat"))
    alpha = gamma / (sums[0] + ridge * sums[1])
    coef_new = coef + alpha[None, :] * direction
    resid_new = resid - alpha[None, :] * image
    weighted_b = (row_weight[:, None] * resid_new).astype(jnp.bfloat16)
    weighted_b = lax.all_gather(weighted_b, "rows", axis=0, tiled=True)
    grad = lax.dot_general(
        feats, weighted_b, (((0,), (0,)), ((), ())), preferred_element_type=jnp.float32
    )
    gradient = grad - ridge[None, :] * coef_new
    gamma_new = lax.psum(jnp.sum(gradient * gradient, axis=0), ("rows", "feat"))
    direction_new = gradient + (gamma_new / gamma)[None, :] * direction
    return (coef_new, resid_new, direction_new, gamma_new)


def solution(mesh):
    return jax.shard_map(
        body,
        mesh=mesh,
        in_specs=(
            P("rows", None),
            P(None, "feat"),
            P("feat"),
            P("rows"),
            P("rows", None),
            P(("feat", "rows"), None),
            P(("feat", "rows"), None),
            P(),
            P(),
        ),
        out_specs=(P(("feat", "rows"), None), P("rows", None), P(("feat", "rows"), None), P()),
        check_vma=False,
    )
```

```python
import math

import jax
import jax.numpy as jnp
from jax import lax
from jax.experimental import pallas as pl
from jax.experimental.pallas import tpu as pltpu
from jax.sharding import PartitionSpec as P

FEAT = 32768


def make_features(block_x, freq_cols, phase_cols):
    scale = math.sqrt(2.0 / FEAT)
    angle = jnp.dot(block_x, freq_cols, preferred_element_type=jnp.float32) + phase_cols[None, :]
    return (scale * jnp.cos(angle)).astype(jnp.bfloat16)


def body(descriptors, freqs, phases, row_weight, resid, coef, direction, ridge, gamma):
    own = coef.shape[0]
    groups = lax.axis_size("feat")
    start = lax.axis_index("rows") * own
    freq_cols = lax.dynamic_slice_in_dim(freqs, start, own, 1)
    phase_cols = lax.dynamic_slice_in_dim(phases, start, own, 0)
    every = lax.all_gather(descriptors, "rows", axis=0, tiled=True)
    feats = make_features(every, freq_cols, phase_cols)
    part = jnp.dot(feats, direction.astype(jnp.bfloat16), preferred_element_type=jnp.float32)
    part = lax.psum_scatter(part, "rows", scatter_dimension=0, tiled=True)
    image = row_weight[:, None] * lax.psum(part, "feat")
    sums = jnp.stack([jnp.sum(image * image, axis=0) / groups, jnp.sum(direction * direction, axis=0)])
    sums = lax.psum(sums, ("rows", "feat"))
    alpha = gamma / (sums[0] + ridge * sums[1])
    coef_new = coef + alpha[None, :] * direction
    resid_new = resid - alpha[None, :] * image
    weighted_b = (row_weight[:, None] * resid_new).astype(jnp.bfloat16)
    weighted_b = lax.all_gather(weighted_b, "rows", axis=0, tiled=True)
    grad = lax.dot_general(
        feats, weighted_b, (((0,), (0,)), ((), ())), preferred_element_type=jnp.float32
    )
    gradient = grad - ridge[None, :] * coef_new
    gamma_new = lax.psum(jnp.sum(gradient * gradient, axis=0), ("rows", "feat"))
    direction_new = gradient + (gamma_new / gamma)[None, :] * direction
    return (coef_new, resid_new, direction_new, gamma_new)


STEPS = 4
SLOTS = 16
MESH = pl.DeviceIdType.MESH
SINE = (0.04908738285303116, -0.32298168540000916, 0.6375077962875366, -0.598044216632843, 0.3088735342025757)


def scaled_cos(angle):
    turns = angle * 0.15915493667125702
    v = 0.25 - jnp.abs(turns - jnp.round(turns))
    s = v * v
    p = SINE[4]
    for c in SINE[3::-1]:
        p = p * s + c
    return p * v


def column(row):
    return jnp.transpose(jnp.broadcast_to(row, (128, 128)))


def kernel(
    desc_ref, freqs_ref, phases_ref, weight_ref, resid_ref, coef_ref, direction_ref, ridge_ref, gamma_ref,
    coef_out, resid_out, direction_out, gamma_out,
    fbuf, descs, freqs_t, dir_t, phase8, phase_b, feats, img, got0, got1, got2, got3,
    wb, grad, grad_got, resid_got, small_out, small_got, local_sem, send, recv,
):
    own = coef_ref.shape[0]
    tiles = own // 256
    r, c = lax.axis_index("rows"), lax.axis_index("feat")
    bits = [lax.rem(r // m, 2) for m in (1, 2, 4, 8)]
    plain = [r + m * (1 - 2 * b) for m, b in zip((1, 2, 4, 8), bits)]
    d = 1 - c
    order = (
        d * plain[0] + c * plain[1],
        d * plain[1] + c * plain[2],
        d * plain[2] + c * plain[0],
        plain[3],
    )

    barrier = pltpu.get_barrier_semaphore()
    pl.semaphore_signal(barrier, inc=1, device_id=(r, 1 - c), device_id_type=MESH)
    for p in plain:
        pl.semaphore_signal(barrier, inc=1, device_id=(p, c), device_id_type=MESH)

    def copy(src, dst, k, rows, core=None):
        return pltpu.make_async_remote_copy(
            src_ref=src, dst_ref=dst, send_sem=send.at[k], recv_sem=recv.at[k],
            device_id=(rows, c if core is None else core), device_id_type=MESH,
        )

    fetch = pltpu.make_async_copy(
        freqs_ref.at[:, pl.ds(pl.multiple_of(r * own, own), own)], fbuf, local_sem
    )
    fetch.start()
    descs[pl.ds(0, 128), :] = desc_ref[pl.ds(pl.multiple_of(c * 128, 128), 128), :]
    phase8[0] = phases_ref[pl.ds(pl.multiple_of(r * 8, 8), 8), :]
    dir_t[0] = jnp.transpose(direction_ref[...]).astype(jnp.bfloat16)
    fetch.wait()
    freqs_t[0] = jnp.transpose(fbuf[...].astype(jnp.float32)).astype(jnp.bfloat16)

    pl.semaphore_wait(barrier, 5)

    def spread(buf, size, k, base):
        return copy(buf.at[pl.ds(0, size)], buf.at[pl.ds(size, size)], base + k, order[3 - k])

    gather = [spread(descs, 128 << k, k, 0) for k in range(STEPS)]
    gather[0].start()
    swap = [
        copy(phase8.at[0], phase8.at[1], 4, r, 1 - c),
        copy(freqs_t.at[0], freqs_t.at[1], 5, r, 1 - c),
        copy(dir_t.at[0], dir_t.at[1], 6, r, 1 - c),
    ]
    for s in swap:
        s.start()

    def expand(h):
        for j in range(8):
            phase_b[h, pl.ds(128 * j, 128), :] = column(phase8[h, pl.ds(j, 1), :])

    expand(0)
    weight = column(weight_ref[pl.ds(c, 1), :])
    direction_sq = jnp.sum(direction_ref[...] * direction_ref[...], axis=0, keepdims=True)
    gather[0].wait()
    gather[1].start()
    swap[0].wait()
    expand(1)
    swap[1].wait()
    swap[2].wait()

    def scatter0(b):
        return copy(img.at[pl.ds(2 * b, 2)], got0.at[pl.ds(2 * (b - 4), 2)], 4 + b, order[0])

    scatter1 = copy(img.at[pl.ds(4, 4)], got1, 12, order[1])

    def block(i, carry):
        @pl.when(i == 1)
        def _():
            gather[1].wait()
            gather[2].start()

        @pl.when(i == 2)
        def _():
            gather[2].wait()
            gather[3].start()

        @pl.when(i == 4)
        def _():
            gather[3].wait()

        far = i // 4
        b = far * (4 + lax.rem(i + 2, 4)) + (1 - far) * i
        x = descs[pl.ds(pl.multiple_of(b * 256, 256), 256), :]
        acc = jnp.zeros((128, 256), jnp.float32)
        for h in range(2):
            for t in range(tiles):
                rows = pl.ds(256 * t, 256)
                a = lax.dot_general(
                    freqs_t[h, rows, :], x, (((1,), (1,)), ((), ())), preferred_element_type=jnp.float32
                )
                ph = phase_b[h, rows, :]
                f = scaled_cos(a + jnp.concatenate([ph, ph], axis=1)).astype(jnp.bfloat16)
                feats[b, h, rows, :] = f
                acc += jnp.dot(dir_t[h, :, rows], f, preferred_element_type=jnp.float32)
        img[2 * b] = acc[:, :128]
        img[2 * b + 1] = acc[:, 128:]

        @pl.when(i >= 4)
        def _():
            scatter0(b).start()

        return carry

    lax.fori_loop(0, 8, block, 0)

    for b in (6, 7):
        scatter0(b).wait()
    for j in range(4, 8):
        img[j] = img[j] + got0[j]
    scatter1.start()
    for b in (4, 5):
        scatter0(b).wait()
    for j in (2, 3, 0, 1):
        img[j] = img[j] + got0[j]
    scatter1.wait()
    for j in (2, 3):
        img[j] = img[j] + got1[j]
    scatter2 = copy(img.at[pl.ds(2, 2)], got2, 13, order[2])
    scatter2.start()
    for j in (0, 1):
        img[j] = img[j] + got1[j]
    scatter2.wait()
    img[1] = img[1] + got2[1]
    scatter3 = copy(img.at[1], got3, 14, order[3])
    scatter3.start()
    img[0] = img[0] + got2[0]
    scatter3.wait()

    def allsum(value, call):
        small = jnp.broadcast_to(value, (8, 128)) if value.shape[0] == 1 else value
        for k in range(5):
            n = 5 * call + k
            small_out[n] = small
            rows, core = (r, 1 - c) if k == 0 else (plain[k - 1], c)
            s = copy(small_out.at[n], small_got.at[n], 15 + n, rows, core)
            s.start()
            s.wait()
            small = small + small_got[n]
        return small

    image = weight * jnp.transpose(img[0] + got3[...])
    image_sq = jnp.sum(image * image, axis=0, keepdims=True)
    first = lax.broadcasted_iota(jnp.int32, (8, 128), 0) == 0
    sums = allsum(jnp.where(first, image_sq, direction_sq), 0)
    ridge, gamma = ridge_ref[...], gamma_ref[...]
    alpha = gamma / (sums[0:1] + ridge * sums[1:2])
    half = pl.ds(pl.multiple_of(c * 128, 128), 128)
    other = pl.ds(pl.multiple_of((1 - c) * 128, 128), 128)
    resid = resid_ref[half, :] - alpha * image
    wb[pl.ds(0, 128), :] = (weight * resid).astype(jnp.bfloat16)
    wgather = [spread(wb, 128 << k, k, 25) for k in range(STEPS)]
    wgather[0].start()
    resid_out[half, :] = resid
    resid_got[0] = resid
    rswap = copy(resid_got.at[0], resid_got.at[1], 29, r, 1 - c)
    rswap.start()
    coef_out[...] = coef_ref[...] + alpha * direction_ref[...]

    def gradient(h, blocks, fresh=False):
        for t in range(tiles):
            rows = pl.ds(256 * t, 256)
            g = None if fresh else grad[h, rows, :]
            for b in blocks:
                p = jnp.dot(feats[b, h, rows, :], wb[pl.ds(256 * b, 256), :], preferred_element_type=jnp.float32)
                g = p if g is None else g + p
            grad[h, rows, :] = g

    for k, blocks in ((0, (0,)), (1, (1,)), (2, (2, 3))):
        wgather[k].wait()
        wgather[k + 1].start()
        for h in (1, 0):
            gradient(h, blocks, fresh=k == 0)
    wgather[3].wait()
    gradient(1, (4, 5, 6, 7))
    gswap = copy(grad.at[1], grad_got, 30, r, 1 - c)
    gswap.start()
    gradient(0, (4, 5, 6, 7))
    rswap.wait()
    resid_out[other, :] = resid_got[1]
    gswap.wait()
    total = grad[0] + grad_got[...] - ridge * coef_out[...]
    grad[0] = total
    gamma_new = allsum(jnp.sum(total * total, axis=0, keepdims=True), 1)[0:1]
    gamma_out[...] = gamma_new
    direction_out[...] = grad[0] + (gamma_new / gamma) * direction_ref[...]


def kernel_body(descriptors, freqs, phases, row_weight, resid, coef, direction, ridge, gamma):
    own, targets = coef.shape
    bf, f32 = jnp.bfloat16, jnp.float32
    vmem = pl.BlockSpec(memory_space=pltpu.VMEM)
    outs = pl.pallas_call(
        kernel,
        out_shape=(
            jax.ShapeDtypeStruct(coef.shape, f32),
            jax.ShapeDtypeStruct(resid.shape, f32),
            jax.ShapeDtypeStruct(direction.shape, f32),
            jax.ShapeDtypeStruct((1, targets), f32),
        ),
        in_specs=[vmem, pl.BlockSpec(memory_space=pl.ANY)] + [vmem] * 7,
        out_specs=(vmem,) * 4,
        scratch_shapes=[
            pltpu.VMEM((128, own), bf),
            pltpu.VMEM((SLOTS * 128, 128), bf),
            pltpu.VMEM((2, own, 128), bf),
            pltpu.VMEM((2, 128, own), bf),
            pltpu.VMEM((2, 8, 128), f32),
            pltpu.VMEM((2, own, 128), f32),
            pltpu.VMEM((SLOTS // 2, 2, own, 256), bf),
            pltpu.VMEM((SLOTS, 128, 128), f32),
            pltpu.VMEM((8, 128, 128), f32),
            pltpu.VMEM((4, 128, 128), f32),
            pltpu.VMEM((2, 128, 128), f32),
            pltpu.VMEM((128, 128), f32),
            pltpu.VMEM((SLOTS * 128, 128), bf),
            pltpu.VMEM((2, own, 128), f32),
            pltpu.VMEM((own, 128), f32),
            pltpu.VMEM((2, 128, 128), f32),
            pltpu.VMEM((10, 8, 128), f32),
            pltpu.VMEM((10, 8, 128), f32),
            pltpu.SemaphoreType.DMA,
            pltpu.SemaphoreType.DMA((31,)),
            pltpu.SemaphoreType.DMA((31,)),
        ],
        compiler_params=pltpu.CompilerParams(
            collective_id=0, has_side_effects=True, vmem_limit_bytes=48 * 1024 * 1024
        ),
    )(
        descriptors, freqs, phases.reshape(-1, 128), row_weight.reshape(2, 128), resid, coef, direction,
        ridge.reshape(1, -1), gamma.reshape(1, -1),
    )
    return outs[0], outs[1], outs[2], outs[3].reshape(-1)


def solution(mesh):
    fits = mesh.shape["rows"] == SLOTS and mesh.shape["feat"] == 2
    return jax.shard_map(
        kernel_body if fits else body,
        mesh=mesh,
        in_specs=(
            P("rows", None),
            P(None, "feat"),
            P("feat"),
            P("rows"),
            P("rows", None),
            P(("feat", "rows"), None),
            P(("feat", "rows"), None),
            P(),
            P(),
        ),
        out_specs=(P(("feat", "rows"), None), P("rows", None), P(("feat", "rows"), None), P()),
        check_vma=False,
    )
```

```python
import math

import jax
import jax.numpy as jnp
from jax import lax
from jax.experimental import pallas as pl
from jax.experimental.pallas import tpu as pltpu
from jax.sharding import PartitionSpec as P

FEAT = 32768


def make_features(block_x, freq_cols, phase_cols):
    scale = math.sqrt(2.0 / FEAT)
    angle = jnp.dot(block_x, freq_cols, preferred_element_type=jnp.float32) + phase_cols[None, :]
    return (scale * jnp.cos(angle)).astype(jnp.bfloat16)


def body(descriptors, freqs, phases, row_weight, resid, coef, direction, ridge, gamma):
    own = coef.shape[0]
    groups = lax.axis_size("feat")
    start = lax.axis_index("rows") * own
    freq_cols = lax.dynamic_slice_in_dim(freqs, start, own, 1)
    phase_cols = lax.dynamic_slice_in_dim(phases, start, own, 0)
    every = lax.all_gather(descriptors, "rows", axis=0, tiled=True)
    feats = make_features(every, freq_cols, phase_cols)
    part = jnp.dot(feats, direction.astype(jnp.bfloat16), preferred_element_type=jnp.float32)
    part = lax.psum_scatter(part, "rows", scatter_dimension=0, tiled=True)
    image = row_weight[:, None] * lax.psum(part, "feat")
    sums = jnp.stack([jnp.sum(image * image, axis=0) / groups, jnp.sum(direction * direction, axis=0)])
    sums = lax.psum(sums, ("rows", "feat"))
    alpha = gamma / (sums[0] + ridge * sums[1])
    coef_new = coef + alpha[None, :] * direction
    resid_new = resid - alpha[None, :] * image
    weighted_b = (row_weight[:, None] * resid_new).astype(jnp.bfloat16)
    weighted_b = lax.all_gather(weighted_b, "rows", axis=0, tiled=True)
    grad = lax.dot_general(
        feats, weighted_b, (((0,), (0,)), ((), ())), preferred_element_type=jnp.float32
    )
    gradient = grad - ridge[None, :] * coef_new
    gamma_new = lax.psum(jnp.sum(gradient * gradient, axis=0), ("rows", "feat"))
    direction_new = gradient + (gamma_new / gamma)[None, :] * direction
    return (coef_new, resid_new, direction_new, gamma_new)


STEPS = 4
SLOTS = 16
MESH = pl.DeviceIdType.MESH
SINE = (0.04908738285303116, -0.32298168540000916, 0.6375077962875366, -0.598044216632843, 0.3088735342025757)


def scaled_cos(angle):
    turns = angle * 0.15915493667125702
    v = 0.25 - jnp.abs(turns - jnp.round(turns))
    s = v * v
    p = SINE[4]
    for c in SINE[3::-1]:
        p = p * s + c
    return p * v


def column(row):
    return jnp.transpose(jnp.broadcast_to(row, (128, 128)))


def kernel(
    desc_ref, freqs_ref, phases_ref, weight_ref, resid_ref, coef_ref, direction_ref, ridge_ref, gamma_ref,
    coef_out, resid_out, direction_out, gamma_out,
    fbuf, dbuf, cbuf, rbuf, wbuf, ridge_buf, gamma_buf,
    descs, freqs_t, dir_t, phase8, phase_b, feats, img, got,
    wb, grad, grad_got, resid_got, small, local_sem, send, recv,
):
    own = coef_ref.shape[0]
    tiles = own // 256
    r, c = lax.axis_index("rows"), lax.axis_index("feat")
    bits = [lax.rem(r // m, 2) for m in (1, 2, 4, 8)]
    x, y, z1, z2 = [m * (1 - 2 * b) for m, b in zip((1, 2, 4, 8), bits)]
    d = 1 - c
    order = (r + d * x + c * y, r + d * y + c * z1, r + d * z1 + c * x, r + z2)
    plane = [(r + i * x + j * y, c + k * (1 - 2 * c)) for j in (0, 1) for i in (0, 1) for k in (0, 1)]
    line = [(r + i * z1 + j * z2, c) for j in (0, 1) for i in (0, 1)]

    barrier = pltpu.get_barrier_semaphore()
    for p in plane[1:] + line[1:]:
        pl.semaphore_signal(barrier, inc=1, device_id=p, device_id_type=MESH)

    half = pl.ds(pl.multiple_of(c * 128, 128), 128)
    other = pl.ds(pl.multiple_of((1 - c) * 128, 128), 128)
    fetches = [
        pltpu.make_async_copy(src, dst, local_sem.at[n])
        for n, (src, dst) in enumerate(
            (
                (desc_ref.at[half], descs.at[pl.ds(0, 128)]),
                (phases_ref.at[pl.ds(pl.multiple_of(r * 8, 8), 8)], phase8.at[0]),
                (freqs_ref.at[:, pl.ds(pl.multiple_of(r * own, own), own)], fbuf),
                (direction_ref, dbuf),
                (weight_ref, wbuf),
                (resid_ref.at[half], rbuf),
                (coef_ref, cbuf),
                (ridge_ref, ridge_buf),
                (gamma_ref, gamma_buf),
            )
        )
    ]
    for f in fetches:
        f.start()

    def copy(src, dst, k, device):
        return pltpu.make_async_remote_copy(
            src_ref=src, dst_ref=dst, send_sem=send.at[k], recv_sem=recv.at[k],
            device_id=device, device_id_type=MESH,
        )

    def level(slot):
        return slot.bit_length() - 1

    def gathered(buf, slot, base):
        k = level(slot)
        return copy(
            buf.at[pl.ds(128 * (slot - (1 << k)), 128)], buf.at[pl.ds(128 * slot, 128)],
            base + slot, (order[3 - k], c),
        )

    def forward(buf, slot, base):
        first = 0 if slot == 0 else level(slot) + 1
        for k in range(first, STEPS):
            gathered(buf, slot + (1 << k), base).start()

    def take(buf, slot, base, pass_on=True):
        gathered(buf, slot, base).wait_recv()
        if pass_on:
            forward(buf, slot, base)

    D, W, S, A, M = 0, 16, 32, 48, 68

    fetches[0].wait()
    fetches[1].wait()
    fetches[2].wait()
    freqs_t[0] = jnp.transpose(fbuf[...].astype(jnp.float32)).astype(jnp.bfloat16)
    fetches[3].wait()
    dir_t[0] = jnp.transpose(dbuf[...]).astype(jnp.bfloat16)
    pl.semaphore_wait(barrier, 10)

    forward(descs, 0, D)
    mate = (r, 1 - c)
    swap = [
        copy(phase8.at[0], phase8.at[1], M, mate),
        copy(freqs_t.at[0], freqs_t.at[1], M + 1, mate),
        copy(dir_t.at[0], dir_t.at[1], M + 2, mate),
    ]
    for s in swap:
        s.start()

    def expand(h):
        for j in range(8):
            phase_b[h, pl.ds(128 * j, 128), :] = column(phase8[h, pl.ds(j, 1), :])

    expand(0)
    for f in fetches[4:]:
        f.wait()
    weight = column(wbuf[pl.ds(c, 1), :])
    direction_sq = jnp.sum(dbuf[...] * dbuf[...], axis=0, keepdims=True)
    take(descs, 1, D)
    take(descs, 2, D)
    swap[0].wait_recv()
    expand(1)
    swap[1].wait_recv()
    swap[2].wait_recv()

    def summed(slot):
        return copy(img.at[slot], got.at[slot], S + slot, (order[3 - level(slot)], c))

    def far(slot):
        return copy(img.at[slot], got.at[slot], S + slot, (order[0], c))

    def collect(slot, tops):
        for k in tops:
            summed(slot + (1 << k)).wait_recv()
        total = img[slot]
        for k in tops:
            total = total + got[slot + (1 << k)]
        if slot:
            img[slot] = total
            summed(slot).start()
        return total

    def block(i, carry):
        @pl.when(i == 1)
        def _():
            for s in (4, 3, 5, 6):
                take(descs, s, D)

        @pl.when(i == 2)
        def _():
            take(descs, 7, D)
            for s in (14, 15):
                take(descs, s, D)

        for step in (3, 4, 5):
            @pl.when(i == step)
            def _():
                for s in (18 - 2 * step, 19 - 2 * step):
                    take(descs, s, D)

        near = 1 - (i + 6) // 8
        b = near * i + (1 - near) * (9 - i)
        rows_b = descs[pl.ds(pl.multiple_of(b * 256, 256), 256), :]
        acc = jnp.zeros((128, 256), jnp.float32)
        for h in range(2):
            for t in range(tiles):
                rows = pl.ds(256 * t, 256)
                a = lax.dot_general(
                    freqs_t[h, rows, :], rows_b, (((1,), (1,)), ((), ())), preferred_element_type=jnp.float32
                )
                ph = phase_b[h, rows, :]
                f = scaled_cos(a + jnp.concatenate([ph, ph], axis=1)).astype(jnp.bfloat16)
                feats[b, h, rows, :] = f
                acc += jnp.dot(dir_t[h, :, rows], f, preferred_element_type=jnp.float32)
        img[2 * b] = acc[:, :128]
        img[2 * b + 1] = acc[:, 128:]

        @pl.when(b >= 4)
        def _():
            far(2 * b + 1).start()
            far(2 * b).start()

        @pl.when(i == 6)
        def _():
            collect(7, (3,))
            collect(6, (3,))

        @pl.when(i == 7)
        def _():
            collect(5, (3,))
            collect(4, (3,))

        return carry

    lax.fori_loop(0, 8, block, 0)
    collect(3, (3, 2))
    collect(2, (3, 2))
    collect(1, (3, 2, 1))
    own_img = collect(0, (3, 2, 1, 0))

    def allsum(value, call):
        for stage, group in ((0, plane), (1, line)):
            small[call, stage, 0] = value
            hops = [
                copy(small.at[call, stage, 0], small.at[call, stage, j], A + 10 * call + 7 * stage + j - 1, group[j])
                for j in range(1, len(group))
            ]
            for p in hops:
                p.start()
            for p in hops:
                p.wait_recv()
            terms = [small[call, stage, j] for j in range(len(group))]
            while len(terms) > 1:
                terms = [terms[j] + terms[j + 1] for j in range(0, len(terms), 2)]
            value = terms[0]
            for p in hops:
                p.wait_send()
        return value

    image = weight * jnp.transpose(own_img)
    image_sq = jnp.sum(image * image, axis=0, keepdims=True)
    first = lax.broadcasted_iota(jnp.int32, (8, 128), 0) == 0
    sums = allsum(jnp.where(first, image_sq, direction_sq), 0)
    ridge, gamma = ridge_buf[...], gamma_buf[...]
    alpha = gamma / (sums[0:1] + ridge * sums[1:2])
    resid = rbuf[...] - alpha * image
    wb[pl.ds(0, 128), :] = (weight * resid).astype(jnp.bfloat16)
    forward(wb, 0, W)
    resid_out[half, :] = resid
    resid_got[0] = resid
    rswap = copy(resid_got.at[0], resid_got.at[1], M + 3, mate)
    rswap.start()
    coef_out[...] = cbuf[...] + alpha * dbuf[...]

    def gradient(h, t, blocks, fresh):
        rows = pl.ds(256 * t, 256)
        g = None if fresh else grad[h, rows, :]
        for b in blocks:
            p = jnp.dot(feats[b, h, rows, :], wb[pl.ds(256 * b, 256), :], preferred_element_type=jnp.float32)
            g = p if g is None else g + p
        grad[h, rows, :] = g

    for s in (1, 2, 4, 3, 5, 6, 7):
        take(wb, s, W)
    for h in (1, 0):
        for t in range(tiles):
            gradient(h, t, (0, 1, 2, 3), True)
    for s in range(8, 16):
        take(wb, s, W, False)
    gswap = [
        copy(grad.at[1, pl.ds(256 * t, 256)], grad_got.at[pl.ds(256 * t, 256)], M + 4 + t, mate)
        for t in range(tiles)
    ]
    for t in range(tiles):
        gradient(1, t, (4, 5, 6, 7), False)
        gswap[t].start()
    for t in range(tiles):
        gradient(0, t, (4, 5, 6, 7), False)
    rswap.wait()
    resid_out[other, :] = resid_got[1]
    squares = jnp.zeros((1, 128), jnp.float32)
    for t in range(tiles):
        gswap[t].wait_recv()
        rows = pl.ds(256 * t, 256)
        total = grad[0, rows, :] + grad_got[rows, :] - ridge * coef_out[rows, :]
        grad[0, rows, :] = total
        squares += jnp.sum(total * total, axis=0, keepdims=True)
    gamma_new = allsum(jnp.broadcast_to(squares, (8, 128)), 1)[0:1]
    gamma_out[...] = gamma_new
    direction_out[...] = grad[0] + (gamma_new / gamma) * dbuf[...]
    for s in range(1, 16):
        gathered(descs, s, D).wait_send()
        gathered(wb, s, W).wait_send()
        summed(s).wait_send()
    for s in swap + gswap:
        s.wait_send()


def kernel_body(descriptors, freqs, phases, row_weight, resid, coef, direction, ridge, gamma):
    own, targets = coef.shape
    bf, f32 = jnp.bfloat16, jnp.float32
    vmem = pl.BlockSpec(memory_space=pltpu.VMEM)
    outs = pl.pallas_call(
        kernel,
        out_shape=(
            jax.ShapeDtypeStruct(coef.shape, f32),
            jax.ShapeDtypeStruct(resid.shape, f32),
            jax.ShapeDtypeStruct(direction.shape, f32),
            jax.ShapeDtypeStruct((1, targets), f32),
        ),
        in_specs=[pl.BlockSpec(memory_space=pltpu.HBM)] * 9,
        out_specs=(vmem,) * 4,
        scratch_shapes=[
            pltpu.VMEM((128, own), bf),
            pltpu.VMEM((own, 128), f32),
            pltpu.VMEM((own, 128), f32),
            pltpu.VMEM((128, 128), f32),
            pltpu.VMEM((2, 128), f32),
            pltpu.VMEM((1, 128), f32),
            pltpu.VMEM((1, 128), f32),
            pltpu.VMEM((SLOTS * 128, 128), bf),
            pltpu.VMEM((2, own, 128), bf),
            pltpu.VMEM((2, 128, own), bf),
            pltpu.VMEM((2, 8, 128), f32),
            pltpu.VMEM((2, own, 128), f32),
            pltpu.VMEM((SLOTS // 2, 2, own, 256), bf),
            pltpu.VMEM((SLOTS, 128, 128), f32),
            pltpu.VMEM((SLOTS, 128, 128), f32),
            pltpu.VMEM((SLOTS * 128, 128), bf),
            pltpu.VMEM((2, own, 128), f32),
            pltpu.VMEM((own, 128), f32),
            pltpu.VMEM((2, 128, 128), f32),
            pltpu.VMEM((2, 2, 8, 8, 128), f32),
            pltpu.SemaphoreType.DMA((9,)),
            pltpu.SemaphoreType.DMA((76,)),
            pltpu.SemaphoreType.DMA((76,)),
        ],
        compiler_params=pltpu.CompilerParams(
            collective_id=0, has_side_effects=True, vmem_limit_bytes=48 * 1024 * 1024
        ),
    )(
        descriptors, freqs, phases.reshape(-1, 128), row_weight.reshape(2, 128), resid, coef, direction,
        ridge.reshape(1, -1), gamma.reshape(1, -1),
    )
    return outs[0], outs[1], outs[2], outs[3].reshape(-1)


def solution(mesh):
    fits = mesh.shape["rows"] == SLOTS and mesh.shape["feat"] == 2
    return jax.shard_map(
        kernel_body if fits else body,
        mesh=mesh,
        in_specs=(
            P("rows", None),
            P(None, "feat"),
            P("feat"),
            P("rows"),
            P("rows", None),
            P(("feat", "rows"), None),
            P(("feat", "rows"), None),
            P(),
            P(),
        ),
        out_specs=(P(("feat", "rows"), None), P("rows", None), P(("feat", "rows"), None), P()),
        check_vma=False,
    )
```

```python
import math

import jax
import jax.numpy as jnp
from jax import lax
from jax.experimental import pallas as pl
from jax.experimental.pallas import tpu as pltpu
from jax.sharding import PartitionSpec as P

FEAT = 32768


def make_features(block_x, freq_cols, phase_cols):
    scale = math.sqrt(2.0 / FEAT)
    angle = jnp.dot(block_x, freq_cols, preferred_element_type=jnp.float32) + phase_cols[None, :]
    return (scale * jnp.cos(angle)).astype(jnp.bfloat16)


def body(descriptors, freqs, phases, row_weight, resid, coef, direction, ridge, gamma):
    own = coef.shape[0]
    groups = lax.axis_size("feat")
    start = lax.axis_index("rows") * own
    freq_cols = lax.dynamic_slice_in_dim(freqs, start, own, 1)
    phase_cols = lax.dynamic_slice_in_dim(phases, start, own, 0)
    every = lax.all_gather(descriptors, "rows", axis=0, tiled=True)
    feats = make_features(every, freq_cols, phase_cols)
    part = jnp.dot(feats, direction.astype(jnp.bfloat16), preferred_element_type=jnp.float32)
    part = lax.psum_scatter(part, "rows", scatter_dimension=0, tiled=True)
    image = row_weight[:, None] * lax.psum(part, "feat")
    sums = jnp.stack([jnp.sum(image * image, axis=0) / groups, jnp.sum(direction * direction, axis=0)])
    sums = lax.psum(sums, ("rows", "feat"))
    alpha = gamma / (sums[0] + ridge * sums[1])
    coef_new = coef + alpha[None, :] * direction
    resid_new = resid - alpha[None, :] * image
    weighted_b = (row_weight[:, None] * resid_new).astype(jnp.bfloat16)
    weighted_b = lax.all_gather(weighted_b, "rows", axis=0, tiled=True)
    grad = lax.dot_general(
        feats, weighted_b, (((0,), (0,)), ((), ())), preferred_element_type=jnp.float32
    )
    gradient = grad - ridge[None, :] * coef_new
    gamma_new = lax.psum(jnp.sum(gradient * gradient, axis=0), ("rows", "feat"))
    direction_new = gradient + (gamma_new / gamma)[None, :] * direction
    return (coef_new, resid_new, direction_new, gamma_new)


STEPS = 4
SLOTS = 16
MESH = pl.DeviceIdType.MESH
TURN = 0.15915493667125702
SINE = (0.04908738285303116, -0.32298168540000916, 0.6375077962875366, -0.598044216632843, 0.3088735342025757)


def scaled_cos(turns):
    v = 0.25 - jnp.abs(turns - jnp.round(turns))
    s = v * v
    p = SINE[4]
    for c in SINE[3::-1]:
        p = p * s + c
    return p * v


def thirds(value):
    a = value.astype(jnp.bfloat16)
    rest = value - a.astype(jnp.float32)
    b = rest.astype(jnp.bfloat16)
    return a, b, (rest - b.astype(jnp.float32)).astype(jnp.bfloat16)


def column(row):
    return jnp.transpose(jnp.broadcast_to(row, (128, 128)))


def kernel(
    desc_ref, freqs_ref, phases_ref, weight_ref, resid_ref, coef_ref, direction_ref, ridge_ref, gamma_ref,
    coef_out, resid_out, direction_out, gamma_out,
    fbuf, dbuf, cbuf, rbuf, wbuf, ridge_buf, gamma_buf,
    descs, freqs_t, dir_t, phase8, turn_t, feats, img, got,
    wb, grad, grad_got, resid_got, small, local_sem, send, recv,
):
    own = coef_ref.shape[0]
    tiles = own // 256
    r, c = lax.axis_index("rows"), lax.axis_index("feat")
    bits = [lax.rem(r // m, 2) for m in (1, 2, 4, 8)]
    x, y, z1, z2 = [m * (1 - 2 * b) for m, b in zip((1, 2, 4, 8), bits)]
    d = 1 - c
    order = (r + d * x + c * y, r + d * y + c * z1, r + d * z1 + c * x, r + z2)
    plane = [(r + i * x + j * y, c + k * (1 - 2 * c)) for j in (0, 1) for i in (0, 1) for k in (0, 1)]
    line = [(r + i * z1 + j * z2, c) for j in (0, 1) for i in (0, 1)]

    barrier = pltpu.get_barrier_semaphore()
    for p in plane[1:] + line[1:]:
        pl.semaphore_signal(barrier, inc=1, device_id=p, device_id_type=MESH)

    half = pl.ds(pl.multiple_of(c * 128, 128), 128)
    other = pl.ds(pl.multiple_of((1 - c) * 128, 128), 128)
    fetches = [
        pltpu.make_async_copy(src, dst, local_sem.at[n])
        for n, (src, dst) in enumerate(
            (
                (desc_ref.at[half], descs.at[pl.ds(0, 128)]),
                (phases_ref.at[pl.ds(pl.multiple_of(r * 8, 8), 8)], phase8.at[0]),
                (freqs_ref.at[:, pl.ds(pl.multiple_of(r * own, own), own)], fbuf),
                (direction_ref, dbuf),
                (weight_ref, wbuf),
                (resid_ref.at[half], rbuf),
                (coef_ref, cbuf),
                (ridge_ref, ridge_buf),
                (gamma_ref, gamma_buf),
            )
        )
    ]
    for f in fetches:
        f.start()

    def copy(src, dst, k, device):
        return pltpu.make_async_remote_copy(
            src_ref=src, dst_ref=dst, send_sem=send.at[k], recv_sem=recv.at[k],
            device_id=device, device_id_type=MESH,
        )

    def level(slot):
        return slot.bit_length() - 1

    def gathered(buf, slot, base):
        k = level(slot)
        return copy(
            buf.at[pl.ds(128 * (slot - (1 << k)), 128)], buf.at[pl.ds(128 * slot, 128)],
            base + slot, (order[3 - k], c),
        )

    def forward(buf, slot, base):
        first = 0 if slot == 0 else level(slot) + 1
        for k in range(first, STEPS):
            gathered(buf, slot + (1 << k), base).start()

    def take(buf, slot, base, pass_on=True):
        gathered(buf, slot, base).wait_recv()
        if pass_on:
            forward(buf, slot, base)

    D, W, S, A, M = 0, 16, 32, 48, 68

    fetches[0].wait()
    fetches[1].wait()
    fetches[2].wait()
    freqs_t[0] = jnp.transpose(fbuf[...].astype(jnp.float32)).astype(jnp.bfloat16)
    fetches[3].wait()
    dir_t[0] = jnp.transpose(dbuf[...]).astype(jnp.bfloat16)
    pl.semaphore_wait(barrier, 10)

    forward(descs, 0, D)
    mate = (r, 1 - c)
    swap = [
        copy(phase8.at[0], phase8.at[1], M, mate),
        copy(freqs_t.at[0], freqs_t.at[1], M + 1, mate),
        copy(dir_t.at[0], dir_t.at[1], M + 2, mate),
    ]
    for s in swap:
        s.start()

    lane = lax.broadcasted_iota(jnp.int32, (128, 128), 1)

    def expand(h):
        for j in range(8):
            rows = pl.ds(128 * j, 128)
            terms = thirds(freqs_t[h, rows, :].astype(jnp.float32) * TURN)
            for n in range(3):
                turn_t[h, rows, pl.ds(128 * n, 128)] = terms[n]
            terms = [t.astype(jnp.float32) for t in thirds(column(phase8[h, pl.ds(j, 1), :]) * TURN)]
            last = jnp.where(lane == 0, terms[0], jnp.where(lane == 1, terms[1], jnp.where(lane == 2, terms[2], 0.0)))
            turn_t[h, rows, pl.ds(384, 128)] = last.astype(jnp.bfloat16)

    expand(0)
    for f in fetches[4:]:
        f.wait()
    weight = column(wbuf[pl.ds(c, 1), :])
    direction_sq = jnp.sum(dbuf[...] * dbuf[...], axis=0, keepdims=True)
    take(descs, 1, D)
    take(descs, 2, D)
    swap[0].wait_recv()
    swap[1].wait_recv()
    expand(1)
    swap[2].wait_recv()

    def summed(slot):
        return copy(img.at[slot], got.at[slot], S + slot, (order[3 - level(slot)], c))

    def far(slot):
        return copy(img.at[slot], got.at[slot], S + slot, (order[0], c))

    def collect(slot, tops):
        for k in tops:
            summed(slot + (1 << k)).wait_recv()
        total = img[slot]
        for k in tops:
            total = total + got[slot + (1 << k)]
        if slot:
            img[slot] = total
            summed(slot).start()
        return total

    def block(i, carry):
        @pl.when(i == 1)
        def _():
            for s in (4, 3, 5, 6):
                take(descs, s, D)

        @pl.when(i == 2)
        def _():
            take(descs, 7, D)
            for s in (14, 15):
                take(descs, s, D)

        for step in (3, 4, 5):
            @pl.when(i == step)
            def _():
                for s in (18 - 2 * step, 19 - 2 * step):
                    take(descs, s, D)

        near = 1 - (i + 6) // 8
        b = near * i + (1 - near) * (9 - i)
        rows_b = descs[pl.ds(pl.multiple_of(b * 256, 256), 256), :]
        rows_b = jnp.concatenate([rows_b, rows_b, rows_b, jnp.ones_like(rows_b)], axis=1)
        acc = jnp.zeros((128, 256), jnp.float32)
        for h in range(2):
            for t in range(tiles):
                rows = pl.ds(256 * t, 256)
                a = lax.dot_general(
                    turn_t[h, rows, :], rows_b, (((1,), (1,)), ((), ())), preferred_element_type=jnp.float32
                )
                f = scaled_cos(a).astype(jnp.bfloat16)
                feats[b, h, rows, :] = f
                acc += jnp.dot(dir_t[h, :, rows], f, preferred_element_type=jnp.float32)
        img[2 * b] = acc[:, :128]
        img[2 * b + 1] = acc[:, 128:]

        @pl.when(b >= 4)
        def _():
            far(2 * b + 1).start()
            far(2 * b).start()

        @pl.when(i == 6)
        def _():
            collect(7, (3,))
            collect(6, (3,))

        @pl.when(i == 7)
        def _():
            collect(5, (3,))
            collect(4, (3,))

        return carry

    lax.fori_loop(0, 8, block, 0)
    collect(3, (3, 2))
    collect(2, (3, 2))
    collect(1, (3, 2, 1))
    own_img = collect(0, (3, 2, 1, 0))

    def allsum(value, call):
        for stage, group in ((0, plane), (1, line)):
            small[call, stage, 0] = value
            hops = [
                copy(small.at[call, stage, 0], small.at[call, stage, j], A + 10 * call + 7 * stage + j - 1, group[j])
                for j in range(1, len(group))
            ]
            for p in hops:
                p.start()
            for p in hops:
                p.wait_recv()
            terms = [small[call, stage, j] for j in range(len(group))]
            while len(terms) > 1:
                terms = [terms[j] + terms[j + 1] for j in range(0, len(terms), 2)]
            value = terms[0]
            for p in hops:
                p.wait_send()
        return value

    image = weight * jnp.transpose(own_img)
    image_sq = jnp.sum(image * image, axis=0, keepdims=True)
    first = lax.broadcasted_iota(jnp.int32, (8, 128), 0) == 0
    sums = allsum(jnp.where(first, image_sq, direction_sq), 0)
    ridge, gamma = ridge_buf[...], gamma_buf[...]
    alpha = gamma / (sums[0:1] + ridge * sums[1:2])
    resid = rbuf[...] - alpha * image
    wb[pl.ds(0, 128), :] = (weight * resid).astype(jnp.bfloat16)
    forward(wb, 0, W)
    resid_out[half, :] = resid
    resid_got[0] = resid
    rswap = copy(resid_got.at[0], resid_got.at[1], M + 3, mate)
    rswap.start()
    coef_out[...] = cbuf[...] + alpha * dbuf[...]

    def gradient(h, t, blocks, fresh):
        rows = pl.ds(256 * t, 256)
        g = None if fresh else grad[h, rows, :]
        for b in blocks:
            p = jnp.dot(feats[b, h, rows, :], wb[pl.ds(256 * b, 256), :], preferred_element_type=jnp.float32)
            g = p if g is None else g + p
        grad[h, rows, :] = g

    for s in (1, 2, 4, 3, 5, 6, 7):
        take(wb, s, W)
    for h in (1, 0):
        for t in range(tiles):
            gradient(h, t, (0, 1, 2, 3), True)
    for s in range(8, 16):
        take(wb, s, W, False)
    gswap = [
        copy(grad.at[1, pl.ds(256 * t, 256)], grad_got.at[pl.ds(256 * t, 256)], M + 4 + t, mate)
        for t in range(tiles)
    ]
    for t in range(tiles):
        gradient(1, t, (4, 5, 6, 7), False)
        gswap[t].start()
    for t in range(tiles):
        gradient(0, t, (4, 5, 6, 7), False)
    rswap.wait()
    resid_out[other, :] = resid_got[1]
    squares = jnp.zeros((1, 128), jnp.float32)
    for t in range(tiles):
        gswap[t].wait_recv()
        rows = pl.ds(256 * t, 256)
        total = grad[0, rows, :] + grad_got[rows, :] - ridge * coef_out[rows, :]
        grad[0, rows, :] = total
        squares += jnp.sum(total * total, axis=0, keepdims=True)
    gamma_new = allsum(jnp.broadcast_to(squares, (8, 128)), 1)[0:1]
    gamma_out[...] = gamma_new
    direction_out[...] = grad[0] + (gamma_new / gamma) * dbuf[...]
    for s in range(1, 16):
        gathered(descs, s, D).wait_send()
        gathered(wb, s, W).wait_send()
        summed(s).wait_send()
    for s in swap + gswap:
        s.wait_send()


def kernel_body(descriptors, freqs, phases, row_weight, resid, coef, direction, ridge, gamma):
    own, targets = coef.shape
    bf, f32 = jnp.bfloat16, jnp.float32
    vmem = pl.BlockSpec(memory_space=pltpu.VMEM)
    outs = pl.pallas_call(
        kernel,
        out_shape=(
            jax.ShapeDtypeStruct(coef.shape, f32),
            jax.ShapeDtypeStruct(resid.shape, f32),
            jax.ShapeDtypeStruct(direction.shape, f32),
            jax.ShapeDtypeStruct((1, targets), f32),
        ),
        in_specs=[pl.BlockSpec(memory_space=pltpu.HBM)] * 9,
        out_specs=(vmem,) * 4,
        scratch_shapes=[
            pltpu.VMEM((128, own), bf),
            pltpu.VMEM((own, 128), f32),
            pltpu.VMEM((own, 128), f32),
            pltpu.VMEM((128, 128), f32),
            pltpu.VMEM((2, 128), f32),
            pltpu.VMEM((1, 128), f32),
            pltpu.VMEM((1, 128), f32),
            pltpu.VMEM((SLOTS * 128, 128), bf),
            pltpu.VMEM((2, own, 128), bf),
            pltpu.VMEM((2, 128, own), bf),
            pltpu.VMEM((2, 8, 128), f32),
            pltpu.VMEM((2, own, 512), bf),
            pltpu.VMEM((SLOTS // 2, 2, own, 256), bf),
            pltpu.VMEM((SLOTS, 128, 128), f32),
            pltpu.VMEM((SLOTS, 128, 128), f32),
            pltpu.VMEM((SLOTS * 128, 128), bf),
            pltpu.VMEM((2, own, 128), f32),
            pltpu.VMEM((own, 128), f32),
            pltpu.VMEM((2, 128, 128), f32),
            pltpu.VMEM((2, 2, 8, 8, 128), f32),
            pltpu.SemaphoreType.DMA((9,)),
            pltpu.SemaphoreType.DMA((76,)),
            pltpu.SemaphoreType.DMA((76,)),
        ],
        compiler_params=pltpu.CompilerParams(
            collective_id=0, has_side_effects=True, vmem_limit_bytes=62 * 1024 * 1024
        ),
    )(
        descriptors, freqs, phases.reshape(-1, 128), row_weight.reshape(2, 128), resid, coef, direction,
        ridge.reshape(1, -1), gamma.reshape(1, -1),
    )
    return outs[0], outs[1], outs[2], outs[3].reshape(-1)


def solution(mesh):
    fits = mesh.shape["rows"] == SLOTS and mesh.shape["feat"] == 2
    return jax.shard_map(
        kernel_body if fits else body,
        mesh=mesh,
        in_specs=(
            P("rows", None),
            P(None, "feat"),
            P("feat"),
            P("rows"),
            P("rows", None),
            P(("feat", "rows"), None),
            P(("feat", "rows"), None),
            P(),
            P(),
        ),
        out_specs=(P(("feat", "rows"), None), P("rows", None), P(("feat", "rows"), None), P()),
        check_vma=False,
    )
```

```python
import math

import jax
import jax.numpy as jnp
from jax import lax
from jax.experimental import pallas as pl
from jax.experimental.pallas import tpu as pltpu
from jax.sharding import PartitionSpec as P

FEAT = 32768


def make_features(block_x, freq_cols, phase_cols):
    scale = math.sqrt(2.0 / FEAT)
    angle = jnp.dot(block_x, freq_cols, preferred_element_type=jnp.float32) + phase_cols[None, :]
    return (scale * jnp.cos(angle)).astype(jnp.bfloat16)


def body(descriptors, freqs, phases, row_weight, resid, coef, direction, ridge, gamma):
    own = coef.shape[0]
    groups = lax.axis_size("feat")
    start = lax.axis_index("rows") * own
    freq_cols = lax.dynamic_slice_in_dim(freqs, start, own, 1)
    phase_cols = lax.dynamic_slice_in_dim(phases, start, own, 0)
    every = lax.all_gather(descriptors, "rows", axis=0, tiled=True)
    feats = make_features(every, freq_cols, phase_cols)
    part = jnp.dot(feats, direction.astype(jnp.bfloat16), preferred_element_type=jnp.float32)
    part = lax.psum_scatter(part, "rows", scatter_dimension=0, tiled=True)
    image = row_weight[:, None] * lax.psum(part, "feat")
    sums = jnp.stack([jnp.sum(image * image, axis=0) / groups, jnp.sum(direction * direction, axis=0)])
    sums = lax.psum(sums, ("rows", "feat"))
    alpha = gamma / (sums[0] + ridge * sums[1])
    coef_new = coef + alpha[None, :] * direction
    resid_new = resid - alpha[None, :] * image
    weighted_b = (row_weight[:, None] * resid_new).astype(jnp.bfloat16)
    weighted_b = lax.all_gather(weighted_b, "rows", axis=0, tiled=True)
    grad = lax.dot_general(
        feats, weighted_b, (((0,), (0,)), ((), ())), preferred_element_type=jnp.float32
    )
    gradient = grad - ridge[None, :] * coef_new
    gamma_new = lax.psum(jnp.sum(gradient * gradient, axis=0), ("rows", "feat"))
    direction_new = gradient + (gamma_new / gamma)[None, :] * direction
    return (coef_new, resid_new, direction_new, gamma_new)


STEPS = 4
SLOTS = 16
MESH = pl.DeviceIdType.MESH
TURN = 0.15915493667125702
SINE = (0.04908738285303116, -0.32298168540000916, 0.6375077962875366, -0.598044216632843, 0.3088735342025757)


def scaled_cos(angle):
    turns = angle * TURN
    v = 0.25 - jnp.abs(turns - ((turns + 12582912.0) - 12582912.0))
    s = v * v
    p = SINE[4]
    for c in SINE[3::-1]:
        p = p * s + c
    return p * v


def thirds(value):
    a = value.astype(jnp.bfloat16)
    rest = value - a.astype(jnp.float32)
    b = rest.astype(jnp.bfloat16)
    return a, b, (rest - b.astype(jnp.float32)).astype(jnp.bfloat16)


def column(row):
    return jnp.transpose(jnp.broadcast_to(row, (128, 128)))


def kernel(
    desc_ref, freqs_ref, phases_ref, weight_ref, resid_ref, coef_ref, direction_ref, ridge_ref, gamma_ref,
    coef_out, resid_out, direction_out, gamma_out,
    fbuf, dbuf, cbuf, rbuf, wbuf, ridge_buf, gamma_buf,
    descs, freqs_t, dir_t, phase8, angle_t, feats, img, got,
    wb, grad, grad_got, resid_got, small, local_sem, send, recv,
):
    own = coef_ref.shape[0]
    tiles = own // 256
    r, c = lax.axis_index("rows"), lax.axis_index("feat")
    bits = [lax.rem(r // m, 2) for m in (1, 2, 4, 8)]
    x, y, z1, z2 = [m * (1 - 2 * b) for m, b in zip((1, 2, 4, 8), bits)]
    d = 1 - c
    order = (r + d * x + c * y, r + d * y + c * z1, r + d * z1 + c * x, r + z2)
    plane = [(r + i * x + j * y, c + k * (1 - 2 * c)) for j in (0, 1) for i in (0, 1) for k in (0, 1)]
    line = [(r + i * z1 + j * z2, c) for j in (0, 1) for i in (0, 1)]

    barrier = pltpu.get_barrier_semaphore()
    for p in plane[1:] + line[1:]:
        pl.semaphore_signal(barrier, inc=1, device_id=p, device_id_type=MESH)

    half = pl.ds(pl.multiple_of(c * 128, 128), 128)
    other = pl.ds(pl.multiple_of((1 - c) * 128, 128), 128)
    fetches = [
        pltpu.make_async_copy(src, dst, local_sem.at[n])
        for n, (src, dst) in enumerate(
            (
                (desc_ref.at[half], descs.at[pl.ds(0, 128)]),
                (phases_ref.at[pl.ds(pl.multiple_of(r * 8, 8), 8)], phase8.at[0]),
                (freqs_ref.at[:, pl.ds(pl.multiple_of(r * own, own), own)], fbuf),
                (direction_ref, dbuf),
                (weight_ref, wbuf),
                (resid_ref.at[half], rbuf),
                (coef_ref, cbuf),
                (ridge_ref, ridge_buf),
                (gamma_ref, gamma_buf),
            )
        )
    ]
    for f in fetches:
        f.start()

    def copy(src, dst, k, device):
        return pltpu.make_async_remote_copy(
            src_ref=src, dst_ref=dst, send_sem=send.at[k], recv_sem=recv.at[k],
            device_id=device, device_id_type=MESH,
        )

    def level(slot):
        return slot.bit_length() - 1

    def gathered(buf, slot, base):
        k = level(slot)
        return copy(
            buf.at[pl.ds(128 * (slot - (1 << k)), 128)], buf.at[pl.ds(128 * slot, 128)],
            base + slot, (order[3 - k], c),
        )

    def forward(buf, slot, base):
        first = 0 if slot == 0 else level(slot) + 1
        for k in range(first, STEPS):
            gathered(buf, slot + (1 << k), base).start()

    def take(buf, slot, base, pass_on=True):
        gathered(buf, slot, base).wait_recv()
        if pass_on:
            forward(buf, slot, base)

    D, W, S, A, M = 0, 16, 32, 48, 68

    fetches[0].wait()
    fetches[1].wait()
    fetches[2].wait()
    freqs_t[0] = jnp.transpose(fbuf[...].astype(jnp.float32)).astype(jnp.bfloat16)
    fetches[3].wait()
    dir_t[0] = jnp.transpose(dbuf[...]).astype(jnp.bfloat16)
    pl.semaphore_wait(barrier, 10)

    forward(descs, 0, D)
    mate = (r, 1 - c)
    swap = [
        copy(phase8.at[0], phase8.at[1], M, mate),
        copy(freqs_t.at[0], freqs_t.at[1], M + 1, mate),
        copy(dir_t.at[0], dir_t.at[1], M + 2, mate),
    ]
    for s in swap:
        s.start()

    lane = lax.broadcasted_iota(jnp.int32, (128, 128), 1)

    def expand(h):
        for j in range(8):
            rows = pl.ds(128 * j, 128)
            angle_t[h, rows, pl.ds(0, 128)] = freqs_t[h, rows, :]
            terms = [t.astype(jnp.float32) for t in thirds(column(phase8[h, pl.ds(j, 1), :]))]
            last = jnp.where(lane == 0, terms[0], jnp.where(lane == 1, terms[1], jnp.where(lane == 2, terms[2], 0.0)))
            angle_t[h, rows, pl.ds(128, 128)] = last.astype(jnp.bfloat16)

    expand(0)
    for f in fetches[4:]:
        f.wait()
    weight = column(wbuf[pl.ds(c, 1), :])
    direction_sq = jnp.sum(dbuf[...] * dbuf[...], axis=0, keepdims=True)
    take(descs, 1, D)
    take(descs, 2, D)
    swap[0].wait_recv()
    swap[1].wait_recv()
    expand(1)
    swap[2].wait_recv()

    def summed(slot):
        return copy(img.at[slot], got.at[slot], S + slot, (order[3 - level(slot)], c))

    def far(slot):
        return copy(img.at[slot], got.at[slot], S + slot, (order[0], c))

    def collect(slot, tops):
        for k in tops:
            summed(slot + (1 << k)).wait_recv()
        total = img[slot]
        for k in tops:
            total = total + got[slot + (1 << k)]
        if slot:
            img[slot] = total
            summed(slot).start()
        return total

    def block(i, carry):
        @pl.when(i == 1)
        def _():
            for s in (4, 3, 5, 6):
                take(descs, s, D)

        @pl.when(i == 2)
        def _():
            take(descs, 7, D)
            for s in (14, 15):
                take(descs, s, D)

        for step in (3, 4, 5):
            @pl.when(i == step)
            def _():
                for s in (18 - 2 * step, 19 - 2 * step):
                    take(descs, s, D)

        near = 1 - (i + 6) // 8
        b = near * i + (1 - near) * (9 - i)
        rows_b = descs[pl.ds(pl.multiple_of(b * 256, 256), 256), :]
        rows_b = jnp.concatenate([rows_b, jnp.ones_like(rows_b)], axis=1)
        acc = jnp.zeros((128, 256), jnp.float32)
        for h in range(2):
            for t in range(tiles):
                rows = pl.ds(256 * t, 256)
                a = lax.dot_general(
                    angle_t[h, rows, :], rows_b, (((1,), (1,)), ((), ())), preferred_element_type=jnp.float32
                )
                f = scaled_cos(a).astype(jnp.bfloat16)
                feats[b, h, rows, :] = f
                acc += jnp.dot(dir_t[h, :, rows], f, preferred_element_type=jnp.float32)
        img[2 * b] = acc[:, :128]
        img[2 * b + 1] = acc[:, 128:]

        @pl.when(b >= 4)
        def _():
            far(2 * b + 1).start()
            far(2 * b).start()

        @pl.when(i == 6)
        def _():
            collect(7, (3,))
            collect(6, (3,))

        @pl.when(i == 7)
        def _():
            collect(5, (3,))
            collect(4, (3,))

        return carry

    lax.fori_loop(0, 8, block, 0)
    collect(3, (3, 2))
    collect(2, (3, 2))
    collect(1, (3, 2, 1))
    own_img = collect(0, (3, 2, 1, 0))

    def allsum(value, call):
        for stage, group in ((0, plane), (1, line)):
            small[call, stage, 0] = value
            hops = [
                copy(small.at[call, stage, 0], small.at[call, stage, j], A + 10 * call + 7 * stage + j - 1, group[j])
                for j in range(1, len(group))
            ]
            for p in hops:
                p.start()
            for p in hops:
                p.wait_recv()
            terms = [small[call, stage, j] for j in range(len(group))]
            while len(terms) > 1:
                terms = [terms[j] + terms[j + 1] for j in range(0, len(terms), 2)]
            value = terms[0]
            for p in hops:
                p.wait_send()
        return value

    image = weight * jnp.transpose(own_img)
    image_sq = jnp.sum(image * image, axis=0, keepdims=True)
    first = lax.broadcasted_iota(jnp.int32, (8, 128), 0) == 0
    sums = allsum(jnp.where(first, image_sq, direction_sq), 0)
    ridge, gamma = ridge_buf[...], gamma_buf[...]
    alpha = gamma / (sums[0:1] + ridge * sums[1:2])
    resid = rbuf[...] - alpha * image
    wb[pl.ds(0, 128), :] = (weight * resid).astype(jnp.bfloat16)
    forward(wb, 0, W)
    resid_out[half, :] = resid
    resid_got[0] = resid
    rswap = copy(resid_got.at[0], resid_got.at[1], M + 3, mate)
    rswap.start()
    coef_out[...] = cbuf[...] + alpha * dbuf[...]

    def gradient(h, t, blocks, fresh):
        rows = pl.ds(256 * t, 256)
        g = None if fresh else grad[h, rows, :]
        for b in blocks:
            p = jnp.dot(feats[b, h, rows, :], wb[pl.ds(256 * b, 256), :], preferred_element_type=jnp.float32)
            g = p if g is None else g + p
        grad[h, rows, :] = g

    for s in (1, 2, 4, 3, 5, 6, 7):
        take(wb, s, W)
    for h in (1, 0):
        for t in range(tiles):
            gradient(h, t, (0, 1, 2, 3), True)
    for s in range(8, 16):
        take(wb, s, W, False)
    gswap = [
        copy(grad.at[1, pl.ds(256 * t, 256)], grad_got.at[pl.ds(256 * t, 256)], M + 4 + t, mate)
        for t in range(tiles)
    ]
    for t in range(tiles):
        gradient(1, t, (4, 5, 6, 7), False)
        gswap[t].start()
    for t in range(tiles):
        gradient(0, t, (4, 5, 6, 7), False)
    rswap.wait()
    resid_out[other, :] = resid_got[1]
    squares = jnp.zeros((1, 128), jnp.float32)
    for t in range(tiles):
        gswap[t].wait_recv()
        rows = pl.ds(256 * t, 256)
        total = grad[0, rows, :] + grad_got[rows, :] - ridge * coef_out[rows, :]
        grad[0, rows, :] = total
        squares += jnp.sum(total * total, axis=0, keepdims=True)
    gamma_new = allsum(jnp.broadcast_to(squares, (8, 128)), 1)[0:1]
    gamma_out[...] = gamma_new
    direction_out[...] = grad[0] + (gamma_new / gamma) * dbuf[...]
    for s in range(1, 16):
        gathered(descs, s, D).wait_send()
        gathered(wb, s, W).wait_send()
        summed(s).wait_send()
    for s in swap + gswap:
        s.wait_send()


def kernel_body(descriptors, freqs, phases, row_weight, resid, coef, direction, ridge, gamma):
    own, targets = coef.shape
    bf, f32 = jnp.bfloat16, jnp.float32
    vmem = pl.BlockSpec(memory_space=pltpu.VMEM)
    outs = pl.pallas_call(
        kernel,
        out_shape=(
            jax.ShapeDtypeStruct(coef.shape, f32),
            jax.ShapeDtypeStruct(resid.shape, f32),
            jax.ShapeDtypeStruct(direction.shape, f32),
            jax.ShapeDtypeStruct((1, targets), f32),
        ),
        in_specs=[pl.BlockSpec(memory_space=pltpu.HBM)] * 9,
        out_specs=(vmem,) * 4,
        scratch_shapes=[
            pltpu.VMEM((128, own), bf),
            pltpu.VMEM((own, 128), f32),
            pltpu.VMEM((own, 128), f32),
            pltpu.VMEM((128, 128), f32),
            pltpu.VMEM((2, 128), f32),
            pltpu.VMEM((1, 128), f32),
            pltpu.VMEM((1, 128), f32),
            pltpu.VMEM((SLOTS * 128, 128), bf),
            pltpu.VMEM((2, own, 128), bf),
            pltpu.VMEM((2, 128, own), bf),
            pltpu.VMEM((2, 8, 128), f32),
            pltpu.VMEM((2, own, 256), bf),
            pltpu.VMEM((SLOTS // 2, 2, own, 256), bf),
            pltpu.VMEM((SLOTS, 128, 128), f32),
            pltpu.VMEM((SLOTS, 128, 128), f32),
            pltpu.VMEM((SLOTS * 128, 128), bf),
            pltpu.VMEM((2, own, 128), f32),
            pltpu.VMEM((own, 128), f32),
            pltpu.VMEM((2, 128, 128), f32),
            pltpu.VMEM((2, 2, 8, 8, 128), f32),
            pltpu.SemaphoreType.DMA((9,)),
            pltpu.SemaphoreType.DMA((76,)),
            pltpu.SemaphoreType.DMA((76,)),
        ],
        compiler_params=pltpu.CompilerParams(
            collective_id=0, has_side_effects=True, vmem_limit_bytes=48 * 1024 * 1024
        ),
    )(
        *(
            pltpu.with_memory_space_constraint(a, pltpu.HBM)
            for a in (
                descriptors, freqs, phases.reshape(-1, 128), row_weight.reshape(2, 128), resid, coef, direction,
                ridge.reshape(1, -1), gamma.reshape(1, -1),
            )
        )
    )
    return outs[0], outs[1], outs[2], outs[3].reshape(-1)


def solution(mesh):
    fits = mesh.shape["rows"] == SLOTS and mesh.shape["feat"] == 2
    return jax.shard_map(
        kernel_body if fits else body,
        mesh=mesh,
        in_specs=(
            P("rows", None),
            P(None, "feat"),
            P("feat"),
            P("rows"),
            P("rows", None),
            P(("feat", "rows"), None),
            P(("feat", "rows"), None),
            P(),
            P(),
        ),
        out_specs=(P(("feat", "rows"), None), P("rows", None), P(("feat", "rows"), None), P()),
        check_vma=False,
    )
```

```python
import math

import jax
import jax.numpy as jnp
from jax import lax
from jax.experimental import pallas as pl
from jax.experimental.pallas import tpu as pltpu
from jax.sharding import PartitionSpec as P

FEAT = 32768


def make_features(block_x, freq_cols, phase_cols):
    scale = math.sqrt(2.0 / FEAT)
    angle = jnp.dot(block_x, freq_cols, preferred_element_type=jnp.float32) + phase_cols[None, :]
    return (scale * jnp.cos(angle)).astype(jnp.bfloat16)


def body(descriptors, freqs, phases, row_weight, resid, coef, direction, ridge, gamma):
    own = coef.shape[0]
    groups = lax.axis_size("feat")
    start = lax.axis_index("rows") * own
    freq_cols = lax.dynamic_slice_in_dim(freqs, start, own, 1)
    phase_cols = lax.dynamic_slice_in_dim(phases, start, own, 0)
    every = lax.all_gather(descriptors, "rows", axis=0, tiled=True)
    feats = make_features(every, freq_cols, phase_cols)
    part = jnp.dot(feats, direction.astype(jnp.bfloat16), preferred_element_type=jnp.float32)
    part = lax.psum_scatter(part, "rows", scatter_dimension=0, tiled=True)
    image = row_weight[:, None] * lax.psum(part, "feat")
    sums = jnp.stack([jnp.sum(image * image, axis=0) / groups, jnp.sum(direction * direction, axis=0)])
    sums = lax.psum(sums, ("rows", "feat"))
    alpha = gamma / (sums[0] + ridge * sums[1])
    coef_new = coef + alpha[None, :] * direction
    resid_new = resid - alpha[None, :] * image
    weighted_b = (row_weight[:, None] * resid_new).astype(jnp.bfloat16)
    weighted_b = lax.all_gather(weighted_b, "rows", axis=0, tiled=True)
    grad = lax.dot_general(
        feats, weighted_b, (((0,), (0,)), ((), ())), preferred_element_type=jnp.float32
    )
    gradient = grad - ridge[None, :] * coef_new
    gamma_new = lax.psum(jnp.sum(gradient * gradient, axis=0), ("rows", "feat"))
    direction_new = gradient + (gamma_new / gamma)[None, :] * direction
    return (coef_new, resid_new, direction_new, gamma_new)


STEPS = 4
SLOTS = 16
MESH = pl.DeviceIdType.MESH
TURN = 0.15915493667125702
SINE = (0.04908738285303116, -0.32298168540000916, 0.6375077962875366, -0.598044216632843, 0.3088735342025757)


def scaled_cos(angle):
    turns = angle * TURN
    v = 0.25 - jnp.abs(turns - ((turns + 12582912.0) - 12582912.0))
    s = v * v
    p = SINE[4]
    for c in SINE[3::-1]:
        p = p * s + c
    return p * v


def thirds(value):
    a = value.astype(jnp.bfloat16)
    rest = value - a.astype(jnp.float32)
    b = rest.astype(jnp.bfloat16)
    return a, b, (rest - b.astype(jnp.float32)).astype(jnp.bfloat16)


def column(row):
    return jnp.transpose(jnp.broadcast_to(row, (128, 128)))


def kernel(
    desc_ref, freqs_ref, phases_ref, weight_ref, resid_ref, coef_ref, direction_ref, ridge_ref, gamma_ref,
    coef_out, resid_out, direction_out, gamma_out,
    fbuf, dbuf, cbuf, rbuf, wbuf, ridge_buf, gamma_buf,
    descs, freqs_t, dir_t, phase8, angle_t, feats, img, got,
    wb, grad, grad_got, resid_got, small, local_sem, send, recv,
):
    own = coef_ref.shape[0]
    tiles = own // 256
    r, c = lax.axis_index("rows"), lax.axis_index("feat")
    bits = [lax.rem(r // m, 2) for m in (1, 2, 4, 8)]
    x, y, z1, z2 = [m * (1 - 2 * b) for m, b in zip((1, 2, 4, 8), bits)]
    d = 1 - c
    order = (r + d * x + c * y, r + d * y + c * z1, r + d * z1 + c * x, r + z2)
    plane = [(r + i * x + j * y, c + k * (1 - 2 * c)) for j in (0, 1) for i in (0, 1) for k in (0, 1)]
    line = [(r + i * z1 + j * z2, c) for j in (0, 1) for i in (0, 1)]

    barrier = pltpu.get_barrier_semaphore()
    for p in plane[1:] + line[1:]:
        pl.semaphore_signal(barrier, inc=1, device_id=p, device_id_type=MESH)

    half = pl.ds(pl.multiple_of(c * 128, 128), 128)
    other = pl.ds(pl.multiple_of((1 - c) * 128, 128), 128)
    fetches = [
        pltpu.make_async_copy(src, dst, local_sem.at[n])
        for n, (src, dst) in enumerate(
            (
                (desc_ref.at[half], descs.at[pl.ds(0, 128)]),
                (phases_ref.at[pl.ds(pl.multiple_of(r * 8, 8), 8)], phase8.at[0]),
                (freqs_ref.at[:, pl.ds(pl.multiple_of(r * own, own), own)], fbuf),
                (direction_ref, dbuf),
                (weight_ref, wbuf),
                (resid_ref.at[half], rbuf),
                (coef_ref, cbuf),
                (ridge_ref, ridge_buf),
                (gamma_ref, gamma_buf),
            )
        )
    ]
    for f in fetches:
        f.start()

    def copy(src, dst, k, device):
        return pltpu.make_async_remote_copy(
            src_ref=src, dst_ref=dst, send_sem=send.at[k], recv_sem=recv.at[k],
            device_id=device, device_id_type=MESH,
        )

    def level(slot):
        return slot.bit_length() - 1

    def gathered(buf, slot, base):
        k = level(slot)
        return copy(
            buf.at[pl.ds(128 * (slot - (1 << k)), 128)], buf.at[pl.ds(128 * slot, 128)],
            base + slot, (order[3 - k], c),
        )

    def forward(buf, slot, base):
        first = 0 if slot == 0 else level(slot) + 1
        for k in range(first, STEPS):
            gathered(buf, slot + (1 << k), base).start()

    def take(buf, slot, base, pass_on=True):
        gathered(buf, slot, base).wait_recv()
        if pass_on:
            forward(buf, slot, base)

    D, W, S, A, M = 0, 16, 32, 48, 68

    fetches[0].wait()
    fetches[1].wait()
    fetches[2].wait()
    freqs_t[0] = jnp.transpose(fbuf[...].astype(jnp.float32)).astype(jnp.bfloat16)
    fetches[3].wait()
    dir_t[0] = jnp.transpose(dbuf[...]).astype(jnp.bfloat16)
    pl.semaphore_wait(barrier, 10)

    forward(descs, 0, D)
    mate = (r, 1 - c)
    swap = [
        copy(phase8.at[0], phase8.at[1], M, mate),
        copy(freqs_t.at[0], freqs_t.at[1], M + 1, mate),
        copy(dir_t.at[0], dir_t.at[1], M + 2, mate),
    ]
    for s in swap:
        s.start()

    lane = lax.broadcasted_iota(jnp.int32, (128, 128), 1)

    def expand(h):
        for j in range(8):
            rows = pl.ds(128 * j, 128)
            angle_t[h, rows, pl.ds(0, 128)] = freqs_t[h, rows, :]
            terms = [t.astype(jnp.float32) for t in thirds(column(phase8[h, pl.ds(j, 1), :]))]
            last = jnp.where(lane == 0, terms[0], jnp.where(lane == 1, terms[1], jnp.where(lane == 2, terms[2], 0.0)))
            angle_t[h, rows, pl.ds(128, 128)] = last.astype(jnp.bfloat16)

    expand(0)
    for f in fetches[4:]:
        f.wait()
    weight = column(wbuf[pl.ds(c, 1), :])
    direction_sq = jnp.sum(dbuf[...] * dbuf[...], axis=0, keepdims=True)
    take(descs, 1, D)
    take(descs, 2, D)
    swap[0].wait_recv()
    swap[1].wait_recv()
    expand(1)
    swap[2].wait_recv()

    def summed(slot):
        return copy(img.at[slot], got.at[slot], S + slot, (order[3 - level(slot)], c))

    def far(slot):
        return copy(img.at[slot], got.at[slot], S + slot, (order[0], c))

    def collect(slot, tops):
        for k in tops:
            summed(slot + (1 << k)).wait_recv()
        total = img[slot]
        for k in tops:
            total = total + got[slot + (1 << k)]
        if slot:
            img[slot] = total
            summed(slot).start()
        return total

    def block(i, carry):
        @pl.when(i == 1)
        def _():
            for s in (4, 3, 5, 6):
                take(descs, s, D)

        @pl.when(i == 2)
        def _():
            take(descs, 7, D)
            for s in (14, 15):
                take(descs, s, D)

        for step in (3, 4, 5):
            @pl.when(i == step)
            def _():
                for s in (18 - 2 * step, 19 - 2 * step):
                    take(descs, s, D)

        near = 1 - (i + 6) // 8
        b = near * i + (1 - near) * (9 - i)
        rows_b = descs[pl.ds(pl.multiple_of(b * 256, 256), 256), :]
        turned = jnp.transpose(rows_b.astype(jnp.float32)).astype(jnp.bfloat16)
        turned = jnp.concatenate([turned, jnp.ones_like(turned)], axis=0)
        acc = jnp.zeros((128, 256), jnp.float32)
        for h in range(2):
            for t in range(own // 512):
                rows = pl.ds(512 * t, 512)
                a = jnp.dot(angle_t[h, rows, :], turned, preferred_element_type=jnp.float32)
                f = scaled_cos(a).astype(jnp.bfloat16)
                feats[b, h, rows, :] = f
                acc += jnp.dot(dir_t[h, :, rows], f, preferred_element_type=jnp.float32)
        img[2 * b] = acc[:, :128]
        img[2 * b + 1] = acc[:, 128:]

        @pl.when(b >= 4)
        def _():
            far(2 * b + 1).start()
            far(2 * b).start()

        @pl.when(i == 6)
        def _():
            collect(7, (3,))
            collect(6, (3,))

        @pl.when(i == 7)
        def _():
            collect(5, (3,))
            collect(4, (3,))

        return carry

    lax.fori_loop(0, 8, block, 0)
    collect(3, (3, 2))
    collect(2, (3, 2))
    collect(1, (3, 2, 1))
    own_img = collect(0, (3, 2, 1, 0))

    def allsum(value, call):
        for stage, group in ((0, plane), (1, line)):
            small[call, stage, 0] = value
            hops = [
                copy(small.at[call, stage, 0], small.at[call, stage, j], A + 10 * call + 7 * stage + j - 1, group[j])
                for j in range(1, len(group))
            ]
            for p in hops:
                p.start()
            for p in hops:
                p.wait_recv()
            terms = [small[call, stage, j] for j in range(len(group))]
            while len(terms) > 1:
                terms = [terms[j] + terms[j + 1] for j in range(0, len(terms), 2)]
            value = terms[0]
            for p in hops:
                p.wait_send()
        return value

    image = weight * jnp.transpose(own_img)
    image_sq = jnp.sum(image * image, axis=0, keepdims=True)
    first = lax.broadcasted_iota(jnp.int32, (8, 128), 0) == 0
    sums = allsum(jnp.where(first, image_sq, direction_sq), 0)
    ridge, gamma = ridge_buf[...], gamma_buf[...]
    alpha = gamma / (sums[0:1] + ridge * sums[1:2])
    resid = rbuf[...] - alpha * image
    wb[pl.ds(0, 128), :] = (weight * resid).astype(jnp.bfloat16)
    forward(wb, 0, W)
    resid_out[half, :] = resid
    resid_got[0] = resid
    rswap = copy(resid_got.at[0], resid_got.at[1], M + 3, mate)
    rswap.start()
    coef_out[...] = cbuf[...] + alpha * dbuf[...]
    for s in range(1, 16):
        gathered(descs, s, D).wait_send()
        summed(s).wait_send()
    for s in swap:
        s.wait_send()

    def gradient(h, t, blocks, fresh):
        rows = pl.ds(256 * t, 256)
        g = None if fresh else grad[h, rows, :]
        for b in blocks:
            p = jnp.dot(feats[b, h, rows, :], wb[pl.ds(256 * b, 256), :], preferred_element_type=jnp.float32)
            g = p if g is None else g + p
        grad[h, rows, :] = g

    for s in (1, 2, 4, 3, 5, 6, 7):
        take(wb, s, W)
    for h in (1, 0):
        for t in range(tiles):
            gradient(h, t, (0, 1, 2, 3), True)
    for s in range(8, 16):
        take(wb, s, W, False)
    gswap = [
        copy(grad.at[1, pl.ds(256 * t, 256)], grad_got.at[pl.ds(256 * t, 256)], M + 4 + t, mate)
        for t in range(tiles)
    ]
    for t in range(tiles):
        gradient(1, t, (4, 5, 6, 7), False)
        gswap[t].start()
    for t in range(tiles):
        gradient(0, t, (4, 5, 6, 7), False)
    for s in range(1, 16):
        gathered(wb, s, W).wait_send()
    rswap.wait()
    resid_out[other, :] = resid_got[1]
    squares = jnp.zeros((1, 128), jnp.float32)
    for t in range(tiles):
        gswap[t].wait()
        rows = pl.ds(256 * t, 256)
        total = grad[0, rows, :] + grad_got[rows, :] - ridge * coef_out[rows, :]
        grad[0, rows, :] = total
        squares += jnp.sum(total * total, axis=0, keepdims=True)
    gamma_new = allsum(jnp.broadcast_to(squares, (8, 128)), 1)[0:1]
    gamma_out[...] = gamma_new
    direction_out[...] = grad[0] + (gamma_new / gamma) * dbuf[...]


def kernel_body(descriptors, freqs, phases, row_weight, resid, coef, direction, ridge, gamma):
    own, targets = coef.shape
    bf, f32 = jnp.bfloat16, jnp.float32
    vmem = pl.BlockSpec(memory_space=pltpu.VMEM)
    outs = pl.pallas_call(
        kernel,
        out_shape=(
            jax.ShapeDtypeStruct(coef.shape, f32),
            jax.ShapeDtypeStruct(resid.shape, f32),
            jax.ShapeDtypeStruct(direction.shape, f32),
            jax.ShapeDtypeStruct((1, targets), f32),
        ),
        in_specs=[pl.BlockSpec(memory_space=pltpu.HBM)] * 9,
        out_specs=(vmem,) * 4,
        scratch_shapes=[
            pltpu.VMEM((128, own), bf),
            pltpu.VMEM((own, 128), f32),
            pltpu.VMEM((own, 128), f32),
            pltpu.VMEM((128, 128), f32),
            pltpu.VMEM((2, 128), f32),
            pltpu.VMEM((1, 128), f32),
            pltpu.VMEM((1, 128), f32),
            pltpu.VMEM((SLOTS * 128, 128), bf),
            pltpu.VMEM((2, own, 128), bf),
            pltpu.VMEM((2, 128, own), bf),
            pltpu.VMEM((2, 8, 128), f32),
            pltpu.VMEM((2, own, 256), bf),
            pltpu.VMEM((SLOTS // 2, 2, own, 256), bf),
            pltpu.VMEM((SLOTS, 128, 128), f32),
            pltpu.VMEM((SLOTS, 128, 128), f32),
            pltpu.VMEM((SLOTS * 128, 128), bf),
            pltpu.VMEM((2, own, 128), f32),
            pltpu.VMEM((own, 128), f32),
            pltpu.VMEM((2, 128, 128), f32),
            pltpu.VMEM((2, 2, 8, 8, 128), f32),
            pltpu.SemaphoreType.DMA((9,)),
            pltpu.SemaphoreType.DMA((76,)),
            pltpu.SemaphoreType.DMA((76,)),
        ],
        compiler_params=pltpu.CompilerParams(
            collective_id=0, has_side_effects=True, vmem_limit_bytes=48 * 1024 * 1024
        ),
    )(
        *(
            pltpu.with_memory_space_constraint(a, pltpu.HBM)
            for a in (
                descriptors, freqs, phases.reshape(-1, 128), row_weight.reshape(2, 128), resid, coef, direction,
                ridge.reshape(1, -1), gamma.reshape(1, -1),
            )
        )
    )
    return outs[0], outs[1], outs[2], outs[3].reshape(-1)


def solution(mesh):
    fits = mesh.shape["rows"] == SLOTS and mesh.shape["feat"] == 2
    return jax.shard_map(
        kernel_body if fits else body,
        mesh=mesh,
        in_specs=(
            P("rows", None),
            P(None, "feat"),
            P("feat"),
            P("rows"),
            P("rows", None),
            P(("feat", "rows"), None),
            P(("feat", "rows"), None),
            P(),
            P(),
        ),
        out_specs=(P(("feat", "rows"), None), P("rows", None), P(("feat", "rows"), None), P()),
        check_vma=False,
    )
```

```python
import math

import jax
import jax.numpy as jnp
from jax import lax
from jax.experimental import pallas as pl
from jax.experimental.pallas import tpu as pltpu
from jax.sharding import PartitionSpec as P

FEAT = 32768


def make_features(block_x, freq_cols, phase_cols):
    scale = math.sqrt(2.0 / FEAT)
    angle = jnp.dot(block_x, freq_cols, preferred_element_type=jnp.float32) + phase_cols[None, :]
    return (scale * jnp.cos(angle)).astype(jnp.bfloat16)


def body(descriptors, freqs, phases, row_weight, resid, coef, direction, ridge, gamma):
    own = coef.shape[0]
    groups = lax.axis_size("feat")
    start = lax.axis_index("rows") * own
    freq_cols = lax.dynamic_slice_in_dim(freqs, start, own, 1)
    phase_cols = lax.dynamic_slice_in_dim(phases, start, own, 0)
    every = lax.all_gather(descriptors, "rows", axis=0, tiled=True)
    feats = make_features(every, freq_cols, phase_cols)
    part = jnp.dot(feats, direction.astype(jnp.bfloat16), preferred_element_type=jnp.float32)
    part = lax.psum_scatter(part, "rows", scatter_dimension=0, tiled=True)
    image = row_weight[:, None] * lax.psum(part, "feat")
    sums = jnp.stack([jnp.sum(image * image, axis=0) / groups, jnp.sum(direction * direction, axis=0)])
    sums = lax.psum(sums, ("rows", "feat"))
    alpha = gamma / (sums[0] + ridge * sums[1])
    coef_new = coef + alpha[None, :] * direction
    resid_new = resid - alpha[None, :] * image
    weighted_b = (row_weight[:, None] * resid_new).astype(jnp.bfloat16)
    weighted_b = lax.all_gather(weighted_b, "rows", axis=0, tiled=True)
    grad = lax.dot_general(
        feats, weighted_b, (((0,), (0,)), ((), ())), preferred_element_type=jnp.float32
    )
    gradient = grad - ridge[None, :] * coef_new
    gamma_new = lax.psum(jnp.sum(gradient * gradient, axis=0), ("rows", "feat"))
    direction_new = gradient + (gamma_new / gamma)[None, :] * direction
    return (coef_new, resid_new, direction_new, gamma_new)


STEPS = 4
SLOTS = 16
MESH = pl.DeviceIdType.MESH
TURN = 0.15915493667125702
SINE = (0.04908738285303116, -0.32298168540000916, 0.6375077962875366, -0.598044216632843, 0.3088735342025757)


def scaled_cos(angle):
    turns = angle * TURN
    v = 0.25 - jnp.abs(turns - ((turns + 12582912.0) - 12582912.0))
    s = v * v
    p = SINE[4]
    for c in SINE[3::-1]:
        p = p * s + c
    return p * v


def thirds(value):
    a = value.astype(jnp.bfloat16)
    rest = value - a.astype(jnp.float32)
    b = rest.astype(jnp.bfloat16)
    return a, b, (rest - b.astype(jnp.float32)).astype(jnp.bfloat16)


def column(row):
    return jnp.transpose(jnp.broadcast_to(row, (128, 128)))


def kernel(
    desc_ref, freqs_ref, phases_ref, weight_ref, resid_ref, coef_ref, direction_ref, ridge_ref, gamma_ref,
    coef_out, resid_out, direction_out, gamma_out,
    fbuf, dbuf, cbuf, rbuf, wbuf, ridge_buf, gamma_buf,
    descs, freqs_t, dir_t, phase8, angle_t, feats, img, got,
    wb, grad, grad_got, resid_got, small, local_sem, send, recv,
):
    own = coef_ref.shape[0]
    tiles = own // 256
    r, c = lax.axis_index("rows"), lax.axis_index("feat")
    bits = [lax.rem(r // m, 2) for m in (1, 2, 4, 8)]
    x, y, z1, z2 = [m * (1 - 2 * b) for m, b in zip((1, 2, 4, 8), bits)]
    d = 1 - c
    order = (r + d * x + c * y, r + d * y + c * z1, r + d * z1 + c * x, r + z2)
    both = (0, 1)
    everyone = [
        (r + i * x + j * y + k * z1 + n * z2, c + m * (1 - 2 * c))
        for n in both for k in both for j in both for i in both for m in both
    ]

    barrier = pltpu.get_barrier_semaphore()
    for p in everyone[1:]:
        pl.semaphore_signal(barrier, inc=1, device_id=p, device_id_type=MESH)

    half = pl.ds(pl.multiple_of(c * 128, 128), 128)
    other = pl.ds(pl.multiple_of((1 - c) * 128, 128), 128)
    fetches = [
        pltpu.make_async_copy(src, dst, local_sem.at[n])
        for n, (src, dst) in enumerate(
            (
                (desc_ref.at[half], descs.at[pl.ds(0, 128)]),
                (phases_ref.at[pl.ds(pl.multiple_of(r * 8, 8), 8)], phase8.at[0]),
                (freqs_ref.at[:, pl.ds(pl.multiple_of(r * own, own), own)], fbuf),
                (direction_ref, dbuf),
                (weight_ref, wbuf),
                (resid_ref.at[half], rbuf),
                (coef_ref, cbuf),
                (ridge_ref, ridge_buf),
                (gamma_ref, gamma_buf),
            )
        )
    ]
    for f in fetches:
        f.start()

    def copy(src, dst, k, device):
        return pltpu.make_async_remote_copy(
            src_ref=src, dst_ref=dst, send_sem=send.at[k], recv_sem=recv.at[k],
            device_id=device, device_id_type=MESH,
        )

    def level(slot):
        return slot.bit_length() - 1

    def gathered(buf, slot, base):
        k = level(slot)
        return copy(
            buf.at[pl.ds(128 * (slot - (1 << k)), 128)], buf.at[pl.ds(128 * slot, 128)],
            base + slot, (order[3 - k], c),
        )

    def forward(buf, slot, base):
        first = 0 if slot == 0 else level(slot) + 1
        for k in range(first, STEPS):
            gathered(buf, slot + (1 << k), base).start()

    def take(buf, slot, base, pass_on=True):
        gathered(buf, slot, base).wait_recv()
        if pass_on:
            forward(buf, slot, base)

    D, W, S, A, M = 0, 16, 32, 48, 110

    fetches[0].wait()
    fetches[1].wait()
    fetches[2].wait()
    freqs_t[0] = jnp.transpose(fbuf[...].astype(jnp.float32)).astype(jnp.bfloat16)
    fetches[3].wait()
    dir_t[0] = jnp.transpose(dbuf[...]).astype(jnp.bfloat16)
    pl.semaphore_wait(barrier, 31)

    forward(descs, 0, D)
    mate = (r, 1 - c)
    swap = [
        copy(phase8.at[0], phase8.at[1], M, mate),
        copy(freqs_t.at[0], freqs_t.at[1], M + 1, mate),
        copy(dir_t.at[0], dir_t.at[1], M + 2, mate),
    ]
    for s in swap:
        s.start()

    lane = lax.broadcasted_iota(jnp.int32, (128, 128), 1)

    def expand(h):
        for j in range(8):
            rows = pl.ds(128 * j, 128)
            angle_t[h, rows, pl.ds(0, 128)] = freqs_t[h, rows, :]
            terms = [t.astype(jnp.float32) for t in thirds(column(phase8[h, pl.ds(j, 1), :]))]
            last = jnp.where(lane == 0, terms[0], jnp.where(lane == 1, terms[1], jnp.where(lane == 2, terms[2], 0.0)))
            angle_t[h, rows, pl.ds(128, 128)] = last.astype(jnp.bfloat16)

    expand(0)
    for f in fetches[4:]:
        f.wait()
    weight = column(wbuf[pl.ds(c, 1), :])
    direction_sq = jnp.sum(dbuf[...] * dbuf[...], axis=0, keepdims=True)
    take(descs, 1, D)
    take(descs, 2, D)
    swap[0].wait_recv()
    swap[1].wait_recv()
    expand(1)
    swap[2].wait_recv()

    def summed(slot):
        return copy(img.at[slot], got.at[slot], S + slot, (order[3 - level(slot)], c))

    def far(slot):
        return copy(img.at[slot], got.at[slot], S + slot, (order[0], c))

    def collect(slot, tops):
        for k in tops:
            summed(slot + (1 << k)).wait_recv()
        total = img[slot]
        for k in tops:
            total = total + got[slot + (1 << k)]
        if slot:
            img[slot] = total
            summed(slot).start()
        return total

    def block(i, carry):
        @pl.when(i == 1)
        def _():
            for s in (4, 3, 5, 6):
                take(descs, s, D)

        @pl.when(i == 2)
        def _():
            take(descs, 7, D)
            for s in (14, 15):
                take(descs, s, D)

        for step in (3, 4, 5):
            @pl.when(i == step)
            def _():
                for s in (18 - 2 * step, 19 - 2 * step):
                    take(descs, s, D)

        near = 1 - (i + 6) // 8
        b = near * i + (1 - near) * (9 - i)
        rows_b = descs[pl.ds(pl.multiple_of(b * 256, 256), 256), :]
        turned = jnp.transpose(rows_b.astype(jnp.float32)).astype(jnp.bfloat16)
        turned = jnp.concatenate([turned, jnp.ones_like(turned)], axis=0)
        acc = jnp.zeros((128, 256), jnp.float32)
        for h in range(2):
            for t in range(own // 512):
                rows = pl.ds(512 * t, 512)
                a = jnp.dot(angle_t[h, rows, :], turned, preferred_element_type=jnp.float32)
                f = scaled_cos(a).astype(jnp.bfloat16)
                feats[b, h, rows, :] = f
                acc += jnp.dot(dir_t[h, :, rows], f, preferred_element_type=jnp.float32)
        img[2 * b] = acc[:, :128]
        img[2 * b + 1] = acc[:, 128:]

        @pl.when(b >= 4)
        def _():
            far(2 * b + 1).start()
            far(2 * b).start()

        @pl.when(i == 6)
        def _():
            collect(7, (3,))
            collect(6, (3,))

        @pl.when(i == 7)
        def _():
            collect(5, (3,))
            collect(4, (3,))

        return carry

    lax.fori_loop(0, 8, block, 0)
    collect(3, (3, 2))
    collect(2, (3, 2))
    collect(1, (3, 2, 1))
    own_img = collect(0, (3, 2, 1, 0))

    def allsum(value, call):
        small[call, 0] = value
        hops = [
            copy(small.at[call, 0], small.at[call, j], A + 31 * call + j - 1, everyone[j])
            for j in range(1, 32)
        ]
        for p in hops:
            p.start()
        for p in hops:
            p.wait_recv()
        terms = [small[call, j] for j in range(32)]
        while len(terms) > 1:
            terms = [terms[j] + terms[j + 1] for j in range(0, len(terms), 2)]
        for p in hops:
            p.wait_send()
        return terms[0]

    image = weight * jnp.transpose(own_img)
    image_sq = jnp.sum(image * image, axis=0, keepdims=True)
    first = lax.broadcasted_iota(jnp.int32, (8, 128), 0) == 0
    sums = allsum(jnp.where(first, image_sq, direction_sq), 0)
    ridge, gamma = ridge_buf[...], gamma_buf[...]
    alpha = gamma / (sums[0:1] + ridge * sums[1:2])
    resid = rbuf[...] - alpha * image
    wb[pl.ds(0, 128), :] = (weight * resid).astype(jnp.bfloat16)
    forward(wb, 0, W)
    resid_out[half, :] = resid
    resid_got[0] = resid
    rswap = copy(resid_got.at[0], resid_got.at[1], M + 3, mate)
    rswap.start()
    coef_out[...] = cbuf[...] + alpha * dbuf[...]
    for s in range(1, 16):
        gathered(descs, s, D).wait_send()
        summed(s).wait_send()
    for s in swap:
        s.wait_send()

    def gradient(h, t, blocks, fresh):
        rows = pl.ds(256 * t, 256)
        g = None if fresh else grad[h, rows, :]
        for b in blocks:
            p = jnp.dot(feats[b, h, rows, :], wb[pl.ds(256 * b, 256), :], preferred_element_type=jnp.float32)
            g = p if g is None else g + p
        grad[h, rows, :] = g

    for s in (1, 2, 4, 3, 5, 6, 7):
        take(wb, s, W)
    for h in (1, 0):
        for t in range(tiles):
            gradient(h, t, (0, 1, 2, 3), True)
    for s in range(8, 16):
        take(wb, s, W, False)
    gswap = [
        copy(grad.at[1, pl.ds(256 * t, 256)], grad_got.at[pl.ds(256 * t, 256)], M + 4 + t, mate)
        for t in range(tiles)
    ]
    for t in range(tiles):
        gradient(1, t, (4, 5, 6, 7), False)
        gswap[t].start()
    for t in range(tiles):
        gradient(0, t, (4, 5, 6, 7), False)
    for s in range(1, 16):
        gathered(wb, s, W).wait_send()
    rswap.wait()
    resid_out[other, :] = resid_got[1]
    squares = jnp.zeros((1, 128), jnp.float32)
    for t in range(tiles):
        gswap[t].wait()
        rows = pl.ds(256 * t, 256)
        total = grad[0, rows, :] + grad_got[rows, :] - ridge * coef_out[rows, :]
        grad[0, rows, :] = total
        squares += jnp.sum(total * total, axis=0, keepdims=True)
    gamma_new = allsum(jnp.broadcast_to(squares, (8, 128)), 1)[0:1]
    gamma_out[...] = gamma_new
    direction_out[...] = grad[0] + (gamma_new / gamma) * dbuf[...]


def kernel_body(descriptors, freqs, phases, row_weight, resid, coef, direction, ridge, gamma):
    own, targets = coef.shape
    bf, f32 = jnp.bfloat16, jnp.float32
    vmem = pl.BlockSpec(memory_space=pltpu.VMEM)
    outs = pl.pallas_call(
        kernel,
        out_shape=(
            jax.ShapeDtypeStruct(coef.shape, f32),
            jax.ShapeDtypeStruct(resid.shape, f32),
            jax.ShapeDtypeStruct(direction.shape, f32),
            jax.ShapeDtypeStruct((1, targets), f32),
        ),
        in_specs=[pl.BlockSpec(memory_space=pltpu.HBM)] * 9,
        out_specs=(vmem,) * 4,
        scratch_shapes=[
            pltpu.VMEM((128, own), bf),
            pltpu.VMEM((own, 128), f32),
            pltpu.VMEM((own, 128), f32),
            pltpu.VMEM((128, 128), f32),
            pltpu.VMEM((2, 128), f32),
            pltpu.VMEM((1, 128), f32),
            pltpu.VMEM((1, 128), f32),
            pltpu.VMEM((SLOTS * 128, 128), bf),
            pltpu.VMEM((2, own, 128), bf),
            pltpu.VMEM((2, 128, own), bf),
            pltpu.VMEM((2, 8, 128), f32),
            pltpu.VMEM((2, own, 256), bf),
            pltpu.VMEM((SLOTS // 2, 2, own, 256), bf),
            pltpu.VMEM((SLOTS, 128, 128), f32),
            pltpu.VMEM((SLOTS, 128, 128), f32),
            pltpu.VMEM((SLOTS * 128, 128), bf),
            pltpu.VMEM((2, own, 128), f32),
            pltpu.VMEM((own, 128), f32),
            pltpu.VMEM((2, 128, 128), f32),
            pltpu.VMEM((2, 32, 8, 128), f32),
            pltpu.SemaphoreType.DMA((9,)),
            pltpu.SemaphoreType.DMA((118,)),
            pltpu.SemaphoreType.DMA((118,)),
        ],
        compiler_params=pltpu.CompilerParams(
            collective_id=0, has_side_effects=True, vmem_limit_bytes=48 * 1024 * 1024
        ),
    )(
        *(
            pltpu.with_memory_space_constraint(a, pltpu.HBM)
            for a in (
                descriptors, freqs, phases.reshape(-1, 128), row_weight.reshape(2, 128), resid, coef, direction,
                ridge.reshape(1, -1), gamma.reshape(1, -1),
            )
        )
    )
    return outs[0], outs[1], outs[2], outs[3].reshape(-1)


def solution(mesh):
    fits = mesh.shape["rows"] == SLOTS and mesh.shape["feat"] == 2
    return jax.shard_map(
        kernel_body if fits else body,
        mesh=mesh,
        in_specs=(
            P("rows", None),
            P(None, "feat"),
            P("feat"),
            P("rows"),
            P("rows", None),
            P(("feat", "rows"), None),
            P(("feat", "rows"), None),
            P(),
            P(),
        ),
        out_specs=(P(("feat", "rows"), None), P("rows", None), P(("feat", "rows"), None), P()),
        check_vma=False,
    )
```

```python
import math

import jax
import jax.numpy as jnp
from jax import lax
from jax.experimental import pallas as pl
from jax.experimental.pallas import tpu as pltpu
from jax.sharding import PartitionSpec as P

FEAT = 32768


def make_features(block_x, freq_cols, phase_cols):
    scale = math.sqrt(2.0 / FEAT)
    angle = jnp.dot(block_x, freq_cols, preferred_element_type=jnp.float32) + phase_cols[None, :]
    return (scale * jnp.cos(angle)).astype(jnp.bfloat16)


def body(descriptors, freqs, phases, row_weight, resid, coef, direction, ridge, gamma):
    own = coef.shape[0]
    groups = lax.axis_size("feat")
    start = lax.axis_index("rows") * own
    freq_cols = lax.dynamic_slice_in_dim(freqs, start, own, 1)
    phase_cols = lax.dynamic_slice_in_dim(phases, start, own, 0)
    every = lax.all_gather(descriptors, "rows", axis=0, tiled=True)
    feats = make_features(every, freq_cols, phase_cols)
    part = jnp.dot(feats, direction.astype(jnp.bfloat16), preferred_element_type=jnp.float32)
    part = lax.psum_scatter(part, "rows", scatter_dimension=0, tiled=True)
    image = row_weight[:, None] * lax.psum(part, "feat")
    sums = jnp.stack([jnp.sum(image * image, axis=0) / groups, jnp.sum(direction * direction, axis=0)])
    sums = lax.psum(sums, ("rows", "feat"))
    alpha = gamma / (sums[0] + ridge * sums[1])
    coef_new = coef + alpha[None, :] * direction
    resid_new = resid - alpha[None, :] * image
    weighted_b = (row_weight[:, None] * resid_new).astype(jnp.bfloat16)
    weighted_b = lax.all_gather(weighted_b, "rows", axis=0, tiled=True)
    grad = lax.dot_general(
        feats, weighted_b, (((0,), (0,)), ((), ())), preferred_element_type=jnp.float32
    )
    gradient = grad - ridge[None, :] * coef_new
    gamma_new = lax.psum(jnp.sum(gradient * gradient, axis=0), ("rows", "feat"))
    direction_new = gradient + (gamma_new / gamma)[None, :] * direction
    return (coef_new, resid_new, direction_new, gamma_new)


STEPS = 4
SLOTS = 16
MESH = pl.DeviceIdType.MESH
TURN = 0.15915493667125702
SINE = (0.04908738285303116, -0.32298168540000916, 0.6375077962875366, -0.598044216632843, 0.3088735342025757)


def scaled_cos(angle):
    turns = angle * TURN
    v = 0.25 - jnp.abs(turns - ((turns + 12582912.0) - 12582912.0))
    s = v * v
    p = SINE[4]
    for c in SINE[3::-1]:
        p = p * s + c
    return p * v


def thirds(value):
    a = value.astype(jnp.bfloat16)
    rest = value - a.astype(jnp.float32)
    b = rest.astype(jnp.bfloat16)
    return a, b, (rest - b.astype(jnp.float32)).astype(jnp.bfloat16)


def column(row):
    return jnp.transpose(jnp.broadcast_to(row, (128, 128)))


def kernel(
    desc_ref, freqs_ref, phases_ref, weight_ref, resid_ref, coef_ref, direction_ref, ridge_ref, gamma_ref,
    coef_out, resid_out, direction_out, gamma_out,
    fbuf, dbuf, cbuf, rbuf, wbuf, ridge_buf, gamma_buf,
    descs, freqs_t, dir_t, phase8, angle_t, feats, img, got,
    wb, grad, grad_got, resid_got, small, local_sem, send, recv,
):
    own = coef_ref.shape[0]
    tiles = own // 256
    r, c = lax.axis_index("rows"), lax.axis_index("feat")
    bits = [lax.rem(r // m, 2) for m in (1, 2, 4, 8)]
    x, y, z1, z2 = [m * (1 - 2 * b) for m, b in zip((1, 2, 4, 8), bits)]
    d = 1 - c
    order = (r + d * x + c * y, r + d * y + c * z1, r + d * z1 + c * x, r + z2)
    both = (0, 1)
    everyone = [
        (r + i * x + j * y + k * z1 + n * z2, c + m * (1 - 2 * c))
        for n in both for k in both for j in both for i in both for m in both
    ]

    barrier = pltpu.get_barrier_semaphore()
    for p in everyone[1:]:
        pl.semaphore_signal(barrier, inc=1, device_id=p, device_id_type=MESH)

    half = pl.ds(pl.multiple_of(c * 128, 128), 128)
    other = pl.ds(pl.multiple_of((1 - c) * 128, 128), 128)
    fetches = [
        pltpu.make_async_copy(src, dst, local_sem.at[n])
        for n, (src, dst) in enumerate(
            (
                (desc_ref.at[half], descs.at[pl.ds(0, 128)]),
                (phases_ref.at[pl.ds(pl.multiple_of(r * 8, 8), 8)], phase8.at[0]),
                (freqs_ref.at[:, pl.ds(pl.multiple_of(r * own, own), own)], fbuf),
                (direction_ref, dbuf),
                (weight_ref, wbuf),
                (resid_ref.at[half], rbuf),
                (coef_ref, cbuf),
                (ridge_ref, ridge_buf),
                (gamma_ref, gamma_buf),
            )
        )
    ]
    for f in fetches:
        f.start()

    def copy(src, dst, k, device):
        return pltpu.make_async_remote_copy(
            src_ref=src, dst_ref=dst, send_sem=send.at[k], recv_sem=recv.at[k],
            device_id=device, device_id_type=MESH,
        )

    def level(slot):
        return slot.bit_length() - 1

    def gathered(buf, slot, base):
        move = slot - slot % 4 if slot >= 4 else slot
        to = r
        for k in range(STEPS):
            if move >> k & 1:
                to = to + order[3 - k] - r
        return copy(
            buf.at[pl.ds(128 * (slot - move), 128)], buf.at[pl.ds(128 * slot, 128)], base + slot, (to, c)
        )

    def forward(buf, slot, base):
        near = (1, 2, 3) if slot == 0 else ()
        far_slots = (slot + 4, slot + 8, slot + 12) if slot < 4 else ()
        for n in near + far_slots:
            gathered(buf, n, base).start()

    def take(buf, slot, base, pass_on=True):
        gathered(buf, slot, base).wait_recv()
        if pass_on:
            forward(buf, slot, base)

    D, W, S, A, M = 0, 16, 32, 48, 110

    fetches[0].wait()
    fetches[1].wait()
    fetches[2].wait()
    freqs_t[0] = jnp.transpose(fbuf[...].astype(jnp.float32)).astype(jnp.bfloat16)
    fetches[3].wait()
    dir_t[0] = jnp.transpose(dbuf[...]).astype(jnp.bfloat16)
    pl.semaphore_wait(barrier, 31)

    forward(descs, 0, D)
    mate = (r, 1 - c)
    swap = [
        copy(phase8.at[0], phase8.at[1], M, mate),
        copy(freqs_t.at[0], freqs_t.at[1], M + 1, mate),
        copy(dir_t.at[0], dir_t.at[1], M + 2, mate),
    ]
    for s in swap:
        s.start()

    lane = lax.broadcasted_iota(jnp.int32, (128, 128), 1)

    def expand(h):
        for j in range(8):
            rows = pl.ds(128 * j, 128)
            angle_t[h, rows, pl.ds(0, 128)] = freqs_t[h, rows, :]
            terms = [t.astype(jnp.float32) for t in thirds(column(phase8[h, pl.ds(j, 1), :]))]
            last = jnp.where(lane == 0, terms[0], jnp.where(lane == 1, terms[1], jnp.where(lane == 2, terms[2], 0.0)))
            angle_t[h, rows, pl.ds(128, 128)] = last.astype(jnp.bfloat16)

    expand(0)
    for f in fetches[4:]:
        f.wait()
    weight = column(wbuf[pl.ds(c, 1), :])
    direction_sq = jnp.sum(dbuf[...] * dbuf[...], axis=0, keepdims=True)
    take(descs, 1, D)
    take(descs, 2, D)
    take(descs, 3, D)
    swap[0].wait_recv()
    swap[1].wait_recv()
    expand(1)
    swap[2].wait_recv()

    def summed(slot):
        return copy(img.at[slot], got.at[slot], S + slot, (order[3 - level(slot)], c))

    def far(slot):
        return copy(img.at[slot], got.at[slot], S + slot, (order[0], c))

    def collect(slot, tops):
        for k in tops:
            summed(slot + (1 << k)).wait_recv()
        total = img[slot]
        for k in tops:
            total = total + got[slot + (1 << k)]
        if slot:
            img[slot] = total
            summed(slot).start()
        return total

    def block(i, carry):
        for step in range(2, 8):
            @pl.when(i == step)
            def _():
                for s in (18 - 2 * step, 19 - 2 * step):
                    take(descs, s, D)

        near = 1 - (i + 6) // 8
        b = near * i + (1 - near) * (9 - i)
        rows_b = descs[pl.ds(pl.multiple_of(b * 256, 256), 256), :]
        turned = jnp.transpose(rows_b.astype(jnp.float32)).astype(jnp.bfloat16)
        turned = jnp.concatenate([turned, jnp.ones_like(turned)], axis=0)
        acc = jnp.zeros((128, 256), jnp.float32)
        for h in range(2):
            for t in range(own // 512):
                rows = pl.ds(512 * t, 512)
                a = jnp.dot(angle_t[h, rows, :], turned, preferred_element_type=jnp.float32)
                f = scaled_cos(a).astype(jnp.bfloat16)
                feats[b, h, rows, :] = f
                acc += jnp.dot(dir_t[h, :, rows], f, preferred_element_type=jnp.float32)
        img[2 * b] = acc[:, :128]
        img[2 * b + 1] = acc[:, 128:]

        @pl.when(b >= 4)
        def _():
            far(2 * b + 1).start()
            far(2 * b).start()

        @pl.when(i == 6)
        def _():
            collect(7, (3,))
            collect(6, (3,))

        @pl.when(i == 7)
        def _():
            collect(5, (3,))
            collect(4, (3,))

        return carry

    lax.fori_loop(0, 8, block, 0)
    collect(3, (3, 2))
    collect(2, (3, 2))
    collect(1, (3, 2, 1))
    own_img = collect(0, (3, 2, 1, 0))

    def allsum(value, call):
        small[call, 0] = value
        hops = [
            copy(small.at[call, 0], small.at[call, j], A + 31 * call + j - 1, everyone[j])
            for j in range(1, 32)
        ]
        for p in hops:
            p.start()
        for p in hops:
            p.wait_recv()
        terms = [small[call, j] for j in range(32)]
        while len(terms) > 1:
            terms = [terms[j] + terms[j + 1] for j in range(0, len(terms), 2)]
        for p in hops:
            p.wait_send()
        return terms[0]

    image = weight * jnp.transpose(own_img)
    image_sq = jnp.sum(image * image, axis=0, keepdims=True)
    first = lax.broadcasted_iota(jnp.int32, (8, 128), 0) == 0
    sums = allsum(jnp.where(first, image_sq, direction_sq), 0)
    ridge, gamma = ridge_buf[...], gamma_buf[...]
    alpha = gamma / (sums[0:1] + ridge * sums[1:2])
    resid = rbuf[...] - alpha * image
    wb[pl.ds(0, 128), :] = (weight * resid).astype(jnp.bfloat16)
    forward(wb, 0, W)
    resid_out[half, :] = resid
    resid_got[0] = resid
    rswap = copy(resid_got.at[0], resid_got.at[1], M + 3, mate)
    rswap.start()
    coef_out[...] = cbuf[...] + alpha * dbuf[...]
    for s in range(1, 16):
        gathered(descs, s, D).wait_send()
        summed(s).wait_send()
    for s in swap:
        s.wait_send()

    def gradient(h, t, blocks, fresh):
        rows = pl.ds(256 * t, 256)
        g = None if fresh else grad[h, rows, :]
        for b in blocks:
            p = jnp.dot(feats[b, h, rows, :], wb[pl.ds(256 * b, 256), :], preferred_element_type=jnp.float32)
            g = p if g is None else g + p
        grad[h, rows, :] = g

    for s in range(1, 8):
        take(wb, s, W)
    for h in (1, 0):
        for t in range(tiles):
            gradient(h, t, (0, 1, 2, 3), True)
    for s in range(8, 16):
        take(wb, s, W, False)
    gswap = [
        copy(grad.at[1, pl.ds(256 * t, 256)], grad_got.at[pl.ds(256 * t, 256)], M + 4 + t, mate)
        for t in range(tiles)
    ]
    for t in range(tiles):
        gradient(1, t, (4, 5, 6, 7), False)
        gswap[t].start()
    for t in range(tiles):
        gradient(0, t, (4, 5, 6, 7), False)
    for s in range(1, 16):
        gathered(wb, s, W).wait_send()
    rswap.wait()
    resid_out[other, :] = resid_got[1]
    squares = jnp.zeros((1, 128), jnp.float32)
    for t in range(tiles):
        gswap[t].wait()
        rows = pl.ds(256 * t, 256)
        total = grad[0, rows, :] + grad_got[rows, :] - ridge * coef_out[rows, :]
        grad[0, rows, :] = total
        squares += jnp.sum(total * total, axis=0, keepdims=True)
    gamma_new = allsum(jnp.broadcast_to(squares, (8, 128)), 1)[0:1]
    gamma_out[...] = gamma_new
    direction_out[...] = grad[0] + (gamma_new / gamma) * dbuf[...]


def kernel_body(descriptors, freqs, phases, row_weight, resid, coef, direction, ridge, gamma):
    own, targets = coef.shape
    bf, f32 = jnp.bfloat16, jnp.float32
    vmem = pl.BlockSpec(memory_space=pltpu.VMEM)
    outs = pl.pallas_call(
        kernel,
        out_shape=(
            jax.ShapeDtypeStruct(coef.shape, f32),
            jax.ShapeDtypeStruct(resid.shape, f32),
            jax.ShapeDtypeStruct(direction.shape, f32),
            jax.ShapeDtypeStruct((1, targets), f32),
        ),
        in_specs=[pl.BlockSpec(memory_space=pltpu.HBM)] * 9,
        out_specs=(vmem,) * 4,
        scratch_shapes=[
            pltpu.VMEM((128, own), bf),
            pltpu.VMEM((own, 128), f32),
            pltpu.VMEM((own, 128), f32),
            pltpu.VMEM((128, 128), f32),
            pltpu.VMEM((2, 128), f32),
            pltpu.VMEM((1, 128), f32),
            pltpu.VMEM((1, 128), f32),
            pltpu.VMEM((SLOTS * 128, 128), bf),
            pltpu.VMEM((2, own, 128), bf),
            pltpu.VMEM((2, 128, own), bf),
            pltpu.VMEM((2, 8, 128), f32),
            pltpu.VMEM((2, own, 256), bf),
            pltpu.VMEM((SLOTS // 2, 2, own, 256), bf),
            pltpu.VMEM((SLOTS, 128, 128), f32),
            pltpu.VMEM((SLOTS, 128, 128), f32),
            pltpu.VMEM((SLOTS * 128, 128), bf),
            pltpu.VMEM((2, own, 128), f32),
            pltpu.VMEM((own, 128), f32),
            pltpu.VMEM((2, 128, 128), f32),
            pltpu.VMEM((2, 32, 8, 128), f32),
            pltpu.SemaphoreType.DMA((9,)),
            pltpu.SemaphoreType.DMA((118,)),
            pltpu.SemaphoreType.DMA((118,)),
        ],
        compiler_params=pltpu.CompilerParams(
            collective_id=0, has_side_effects=True, vmem_limit_bytes=48 * 1024 * 1024
        ),
    )(
        *(
            pltpu.with_memory_space_constraint(a, pltpu.HBM)
            for a in (
                descriptors, freqs, phases.reshape(-1, 128), row_weight.reshape(2, 128), resid, coef, direction,
                ridge.reshape(1, -1), gamma.reshape(1, -1),
            )
        )
    )
    return outs[0], outs[1], outs[2], outs[3].reshape(-1)


def solution(mesh):
    fits = mesh.shape["rows"] == SLOTS and mesh.shape["feat"] == 2
    return jax.shard_map(
        kernel_body if fits else body,
        mesh=mesh,
        in_specs=(
            P("rows", None),
            P(None, "feat"),
            P("feat"),
            P("rows"),
            P("rows", None),
            P(("feat", "rows"), None),
            P(("feat", "rows"), None),
            P(),
            P(),
        ),
        out_specs=(P(("feat", "rows"), None), P("rows", None), P(("feat", "rows"), None), P()),
        check_vma=False,
    )
```
